768 devices in a mesh: anc: 24 (over z, core), cand: 32 (over y, x).
Axes of the slice: x: 4, y: 8, z: 12, core: 2. Of those that a mesh axis runs over, the one named last changes fastest.
Arguments:
- anchors: bfloat16 [12288, 1536], P('anc'), may hold values from -0.5 to 0.5
- candidates: bfloat16 [30720, 1536], P('cand'), may hold values from -0.5 to 0.5
- anchor_group: int32 [12288], P('anc'), may hold values from 0 to 15359
- cand_group: int32 [30720], P('cand'), may hold values from 0 to 15359
- anchor_loss_cotangent: float32 [12288], P('anc'), may hold values from -6 to 6
Outputs:
- probe_costs: float32 [12288], P('anc')
- probe_derivatives: float32 [12288, 1536], P(('anc', 'cand'))
- grad_candidates: float32 [30720, 1536], P('cand', 'anc')
The draws below stay inside these ranges and needn't reach their ends.
All inputs are finite; a program needn't handle non-finite values.
Results may differ from the reference program's by a relative error of at most 0.0048.
Values sent between devices are 32-bit elements; how exact they have to be, the bound alone decides.
No kernel may reach another device: no remote copies, remote signals or barrier semaphores. Data moves between devices by JAX's collectives and lax.ppermute only.
A program may use at most 64 MiB of HBM per device.

```python
import math
import jax
import jax.numpy as jnp
import numpy as np
from jax import lax

WIDTH = 1536
ANC_DEV = 512
REFERENCE_COUNT = 12288
POOL = 30720
GROUPS = 15360
N_ANC = 24


def mixed_noise(key, row_total):
    first = jax.random.fold_in(key, 0)
    gauss = jax.random.normal(first, (row_total, WIDTH), jnp.float32)
    return gauss


def topic_rows(key, centers, row_total, lowest, highest):
    keys = jax.random.split(key, 3)
    topics = jax.random.randint(keys[0], (row_total,), 0, 8)
    strength = jnp.exp(jax.random.uniform(keys[1], (row_total, 1), jnp.float32, math.log(lowest), math.log(highest)))
    picked = centers[topics]
    return (strength * picked + mixed_noise(keys[2], row_total)) / jnp.sqrt(jnp.float32(WIDTH))


def anchor_directions(key, lowest, highest):
    centers = jax.random.normal(jax.random.fold_in(key, 5), (8, WIDTH), jnp.float32)
    rows = topic_rows(jax.random.fold_in(key, 7), centers, REFERENCE_COUNT, lowest, highest)
    return (centers, rows)


def scaled_rows(key, rows, smallest, largest):
    factor = jnp.exp(jax.random.uniform(key, (rows.shape[0], 1), jnp.float32, math.log(smallest), math.log(largest)))
    return jnp.clip(factor * rows, -0.5, 0.5).astype(jnp.bfloat16)


def draw_anchors(key, part):
    lowest, highest, smallest = (0.2, 1.2, 0.25)
    centers, rows = anchor_directions(key, lowest, highest)
    key = jax.random.fold_in(key, 11)
    return scaled_rows(key, rows, smallest, 2.0)


def draw_candidates(key, part):
    lowest, highest, smallest = (0.2, 1.2, 0.25)
    centers, anchor_rows = anchor_directions(key, lowest, highest)
    key = jax.random.fold_in(key, 23)
    keys = jax.random.split(key, 5)
    generic = topic_rows(keys[0], centers, POOL, lowest, highest)
    order = jax.random.permutation(keys[1], POOL)
    source = jnp.minimum(order, REFERENCE_COUNT - 1)
    spread = jnp.exp(jax.random.uniform(keys[2], (POOL, 1), jnp.float32, math.log(0.35), math.log(1.3)))
    copies = anchor_rows[source] + spread * mixed_noise(keys[3], POOL) / jnp.sqrt(jnp.float32(WIDTH))
    rows = jnp.where((order < REFERENCE_COUNT)[:, None], copies, generic)
    return scaled_rows(keys[4], rows, smallest, 2.0)


def touch_ends(array, stream_key, low, top_value):
    shape = array.shape
    index_at = [jax.random.randint(jax.random.fold_in(stream_key, axis), (), 0, shape[axis]) for axis in range(len(shape))]
    array = array.at[tuple(index_at)].set(low)
    longest = shape.index(max(shape))
    index_at[longest] = (index_at[longest] + 1) % shape[longest]
    return array.at[tuple(index_at)].set(top_value)


def shard_levels(own_key, dims, cuts, low, high):
    loudness = 1.0
    for dim, parts in cuts:
        heights = jax.random.uniform(jax.random.fold_in(jax.random.fold_in(own_key, 6), dim), (parts,), jnp.float32, low / len(cuts), high / len(cuts))
        loudness = loudness * jnp.repeat(jnp.exp(heights), dims[dim] // parts).reshape((-1,) + (1,) * (len(dims) - 1 - dim))
    return loudness


def cumulative_ranks(number_of, lean):
    portions = [(1 << 20) // math.isqrt(rank ** lean) + 1 for rank in range(1, number_of + 1)]
    deviation = 1 + sum(portions) // (1 << 30)
    return np.cumsum(np.array([max(1, weight // deviation) for weight in portions]))


def ranked_ids(rng, shape, count, slope):
    table = cumulative_ranks(count, slope)
    lot = jax.random.randint(jax.random.fold_in(rng, 1), shape, 0, int(table[count - 1]))
    rank = jnp.searchsorted(jnp.asarray(table, jnp.int32), lot, side="right")
    return jax.random.permutation(jax.random.fold_in(rng, 2), count)[rank].astype(jnp.int32)


def scatter_about(own_key, extent, width, bound, pieces=(), kind=jnp.bfloat16):
    entries = jax.random.normal(own_key, extent, jnp.float32) * width
    if len(pieces) > 0:
        entries = shard_levels(own_key, extent, pieces, -0.22, 0.18) * entries
    return jnp.clip(entries, min=-bound, max=bound).astype(kind)


def setup_inputs(seed: int = 0) -> dict:
    key_of = jax.random.split(jax.random.key(seed), 6)
    return {
        "anchors": draw_anchors(jax.random.fold_in(key_of[5], 71), 0),
        "candidates": draw_candidates(jax.random.fold_in(key_of[5], 71), 0),
        "anchor_group": touch_ends(ranked_ids(key_of[2], (REFERENCE_COUNT,), GROUPS, 1), jax.random.fold_in(key_of[2], 3), 0, GROUPS - 1).astype(jnp.int32),
        "cand_group": touch_ends(ranked_ids(key_of[3], (POOL,), GROUPS, 1), jax.random.fold_in(key_of[3], 3), 0, GROUPS - 1).astype(jnp.int32),
        "anchor_loss_cotangent": scatter_about(key_of[4], (REFERENCE_COUNT,), 1.0, 6.0, ((0, 24),), jnp.float32),
    }


sharpness_scale = 0.05
epsilon = 1e-06

def normalize(rows):
    values = rows.astype(jnp.float32)
    radius = jnp.sqrt(lax.optimization_barrier(jnp.sum(values * values, axis=1, keepdims=True)) + epsilon)
    return (values / radius, radius)

def rescale_onto_sphere(term, unit, radius):
    inner = lax.optimization_barrier(jnp.sum(unit * term, axis=1, keepdims=True))
    return (term - unit * inner) / radius

def reference(anchors, candidates, anchor_group, cand_group, anchor_loss_cotangent):
    probe_direction, probe_length = normalize(anchors)
    pool_member_direction, pool_member_length = normalize(candidates)
    anchor_halfprec = probe_direction.astype(jnp.bfloat16)
    target_reduced_precision = pool_member_direction.astype(jnp.bfloat16)

    def block_step(running_state, inputs):
        query_entry_tile, groups, incoming_adjoint = inputs
        pairwise_logits = jnp.dot(query_entry_tile, target_reduced_precision.T, preferred_element_type=jnp.float32) / sharpness_scale
        logit_exponentials = jnp.exp(pairwise_logits - 1.0 / sharpness_scale)
        denominator_aggregate = lax.optimization_barrier(jnp.sum(logit_exponentials, axis=1))
        matching_indicator = (groups[:, None] == cand_group[None, :]).astype(jnp.float32)
        paired_number = jnp.maximum(lax.optimization_barrier(jnp.sum(matching_indicator, axis=1)), 1.0)
        paired_affinity_aggregate = lax.optimization_barrier(jnp.sum(matching_indicator * pairwise_logits, axis=1))
        probe_costs = 1.0 / sharpness_scale + jnp.log(denominator_aggregate) - paired_affinity_aggregate / paired_number
        normalized_weight_factor = (incoming_adjoint[:, None] * (logit_exponentials / denominator_aggregate[:, None] - matching_indicator / paired_number[:, None]) / sharpness_scale).astype(jnp.bfloat16)
        probe_contribution = jnp.dot(normalized_weight_factor, target_reduced_precision, preferred_element_type=jnp.float32)
        pool_member_contribution = jnp.dot(normalized_weight_factor.T, query_entry_tile, preferred_element_type=jnp.float32)
        return (running_state + pool_member_contribution, (probe_costs, probe_contribution))
    blocks = (anchor_halfprec.reshape(N_ANC, ANC_DEV, WIDTH), anchor_group.reshape(N_ANC, ANC_DEV), anchor_loss_cotangent.reshape(N_ANC, ANC_DEV))
    pool_member_gradient, returned_results = lax.scan(block_step, jnp.zeros((POOL, WIDTH), jnp.float32), blocks)
    probe_costs = returned_results[0].reshape(REFERENCE_COUNT)
    probe_gradient = returned_results[1].reshape(REFERENCE_COUNT, WIDTH)
    return (probe_costs, rescale_onto_sphere(probe_gradient, probe_direction, probe_length), rescale_onto_sphere(pool_member_gradient, pool_member_direction, pool_member_length))
```

```python
import functools

import jax
import jax.numpy as jnp
from jax import lax
from jax.experimental import pallas as pl
from jax.experimental.pallas import tpu as pltpu
from jax.sharding import PartitionSpec as P

SCALE = 20.0
EPS = 1e-06
F32 = jnp.float32
BF16 = jnp.bfloat16
NX, NY = 4, 8
LANES = 128
SLOTS = 16
VMEM = 62 * 2**20


def inverse_radius(values):
    return 1.0 / jnp.sqrt(jnp.sum(values * values, axis=1, keepdims=True) + EPS)


def score_kernel(a_ref, c_ref, ag_ref, cg_ref, an_ref, cn_ref, e_ref, st_ref, ir_ref, acc_ref):
    n = a_ref.shape[0]
    per = n // LANES

    @pl.when(pl.program_id(0) == 0)
    def _():
        for r in range(0, n, 128):
            values = a_ref[r : r + 128, :].astype(F32)
            an_ref[r : r + 128, :] = (values * inverse_radius(values)).astype(BF16)
        acc_ref[...] = jnp.zeros_like(acc_ref)

    values = c_ref[...].astype(F32)
    inv = inverse_radius(values)
    ir_ref[...] = jnp.broadcast_to(inv, ir_ref.shape)
    cn = (values * inv).astype(BF16)
    cn_ref[...] = cn
    scores = SCALE * lax.dot_general(
        cn, an_ref[...], (((1,), (1,)), ((), ())), preferred_element_type=F32
    )
    expo = jnp.exp(scores - SCALE)
    e_ref[...] = expo
    match = cg_ref[...] == ag_ref[...]
    sums = (
        jnp.sum(expo, axis=0, keepdims=True),
        jnp.sum(jnp.where(match, 1.0, 0.0), axis=0, keepdims=True),
        jnp.sum(jnp.where(match, scores, 0.0), axis=0, keepdims=True),
    )
    for k, s in enumerate(sums):
        for j in range(per):
            acc_ref[k * per + j : k * per + j + 1, :] += s[:, j * LANES : (j + 1) * LANES]

    @pl.when(pl.program_id(0) == pl.num_programs(0) - 1)
    def _():
        st_ref[...] = jnp.broadcast_to(acc_ref[...][None], st_ref.shape)


def score_stage(anchors, candidates, ag, cg, copies):
    n, width = anchors.shape
    m = candidates.shape[0]
    steps = 4
    rows = m // steps
    whole = lambda i: (0, 0)
    part = lambda i: (i, 0)
    return pl.pallas_call(
        score_kernel,
        grid=(steps,),
        in_specs=[
            pl.BlockSpec((n, width), whole),
            pl.BlockSpec((rows, width), part),
            pl.BlockSpec((1, n), whole),
            pl.BlockSpec((rows, 1), part),
        ],
        out_specs=[
            pl.BlockSpec((n, width), whole),
            pl.BlockSpec((rows, width), part),
            pl.BlockSpec((rows, n), part),
            pl.BlockSpec((copies, SLOTS, LANES), lambda i: (0, 0, 0)),
            pl.BlockSpec((rows, LANES), part),
        ],
        out_shape=[
            jax.ShapeDtypeStruct((n, width), BF16),
            jax.ShapeDtypeStruct((m, width), BF16),
            jax.ShapeDtypeStruct((m, n), F32),
            jax.ShapeDtypeStruct((copies, SLOTS, LANES), F32),
            jax.ShapeDtypeStruct((m, LANES), F32),
        ],
        scratch_shapes=[pltpu.VMEM((SLOTS, LANES), F32)],
        compiler_params=pltpu.CompilerParams(vmem_limit_bytes=VMEM),
        name="scores",
    )(anchors, candidates, ag, cg)


def candidate_kernel(
    core_ref, st_ref, cot_ref, ag_ref, cg_ref, e_ref, an_ref, c_ref, ir_ref,
    cost_ref, coef_ref, own_ref, oth_ref,
):
    n = ag_ref.shape[1]
    half = e_ref.shape[1]
    per = n // LANES
    st = jnp.sum(st_ref[...], axis=0)
    total, count, positive = (
        jnp.concatenate([st[k * per + j : k * per + j + 1, :] for j in range(per)], axis=1)
        for k in range(3)
    )
    count = jnp.maximum(count, 1.0)
    cost_ref[...] = SCALE + jnp.log(total) - positive / count
    cot = cot_ref[...] * SCALE
    per_total, per_count = 1.0 / total, 1.0 / count
    expo = e_ref[...].reshape(2 * half, n)
    match = cg_ref[...].reshape(2 * half, 1) == ag_ref[...]
    coef = (cot * (expo * per_total - jnp.where(match, per_count, 0.0))).astype(BF16)
    coef_ref[...] = coef.reshape(2, half, n)
    dcn = jnp.dot(coef, an_ref[...], preferred_element_type=F32)
    values = c_ref[...].reshape(2 * half, c_ref.shape[2]).astype(F32)
    inv = ir_ref[...].reshape(2 * half, LANES)[:, :1]
    inner = jnp.sum(values * dcn, axis=1, keepdims=True)
    grad = inv * (dcn - values * (inv * inv * inner))
    low = lax.broadcasted_iota(jnp.int32, (half, LANES), 1) < LANES // 2
    first = core_ref[0] == 0
    for z in range(own_ref.shape[0]):
        top = grad[:half, z * LANES : (z + 1) * LANES]
        bottom = grad[half:, z * LANES : (z + 1) * LANES]
        even = jnp.where(low, top, pltpu.roll(bottom, LANES // 2, 1))
        odd = jnp.where(low, pltpu.roll(top, LANES // 2, 1), bottom)
        own_ref[z] = jnp.where(first, even, odd)
        oth_ref[z] = jnp.where(first, odd, even)


def candidate_stage(core, st, cot, ag, cg, expo, an, candidates, ir):
    copies = st.shape[0]
    n, width = an.shape
    m = candidates.shape[0]
    blocks = width // LANES
    half = m // 2
    steps = 3
    rows = half // steps
    whole = lambda i: (0, 0)
    part = lambda i: (0, i, 0)
    packed = jax.ShapeDtypeStruct((blocks, half, LANES), F32)
    return pl.pallas_call(
        candidate_kernel,
        grid=(steps,),
        in_specs=[
            pl.BlockSpec(memory_space=pltpu.SMEM),
            pl.BlockSpec((copies, SLOTS, LANES), lambda i: (0, 0, 0)),
            pl.BlockSpec((1, n), whole),
            pl.BlockSpec((1, n), whole),
            pl.BlockSpec((2, rows, 1), part),
            pl.BlockSpec((2, rows, n), part),
            pl.BlockSpec((n, width), whole),
            pl.BlockSpec((2, rows, width), part),
            pl.BlockSpec((2, rows, LANES), part),
        ],
        out_specs=[
            pl.BlockSpec((1, n), whole),
            pl.BlockSpec((2, rows, n), part),
            pl.BlockSpec((blocks, rows, LANES), part),
            pl.BlockSpec((blocks, rows, LANES), part),
        ],
        out_shape=[
            jax.ShapeDtypeStruct((1, n), F32),
            jax.ShapeDtypeStruct((2, half, n), BF16),
            packed,
            packed,
        ],
        compiler_params=pltpu.CompilerParams(vmem_limit_bytes=VMEM),
        name="candidate_terms",
    )(
        core, st, cot, ag, cg.reshape(2, half, 1), expo.reshape(2, half, n), an,
        candidates.reshape(2, half, width), ir.reshape(2, half, LANES),
    )


def anchor_kernel(at_ref, coef_ref, cn_ref, xkeep, xsend, ykeep, ysend, scr):
    scr[...] = lax.dot_general(
        coef_ref[...], cn_ref[...], (((0,), (0,)), ((), ())), preferred_element_type=F32
    )
    share, cols = xkeep.shape[3:]
    x0, y0 = at_ref[0], at_ref[1]

    def rows(p, y, q, x):
        place = (2 * p + y) * NX + 2 * q + x
        return pl.ds(pl.multiple_of(place * share, share), share)

    for other in range(2):
        x, y = (x0, y0) if other == 0 else (1 - x0, 1 - y0)
        for p in range(NY // 2):
            for q in range(NX // 2):
                xkeep[other, p, q] = scr[rows(p, y, q, x0), :cols]
                xsend[other, p, q] = scr[rows(p, y, q, 1 - x0), :cols]
                ykeep[other, p, q] = scr[rows(p, y0, q, x), cols:]
                ysend[other, p, q] = scr[rows(p, 1 - y0, q, x), cols:]


def anchor_stage(at, coef, cn, share):
    width = cn.shape[1]
    n = coef.shape[1]
    part = jax.ShapeDtypeStruct((2, NY // 2, NX // 2, share, width // 2), F32)
    vmem = pl.BlockSpec(memory_space=pltpu.VMEM)
    return pl.pallas_call(
        anchor_kernel,
        in_specs=[pl.BlockSpec(memory_space=pltpu.SMEM), vmem, vmem],
        out_specs=[vmem] * 4,
        out_shape=[part] * 4,
        scratch_shapes=[pltpu.VMEM((n, width), F32)],
        compiler_params=pltpu.CompilerParams(vmem_limit_bytes=VMEM),
        name="anchor_terms",
    )(at, coef, cn)


def probe_kernel(t_ref, a_ref, o_ref):
    term = jnp.sum(t_ref[...], axis=0)
    values = a_ref[...].astype(F32)
    inv = inverse_radius(values)
    unit = values * inv
    o_ref[...] = (term - unit * jnp.sum(unit * term, axis=1, keepdims=True)) * inv


def probe_stage(terms, rows):
    return pl.pallas_call(
        probe_kernel,
        out_shape=jax.ShapeDtypeStruct(rows.shape, F32),
        name="probe_derivatives",
    )(terms, rows)


def unpack_kernel(p_ref, o_ref):
    half = p_ref.shape[0]
    t = p_ref[...].T
    o_ref[:, :half] = t[: LANES // 2]
    o_ref[:, half:] = t[LANES // 2 :]


def unpack_stage(packed):
    half = packed.shape[0]
    return pl.pallas_call(
        unpack_kernel,
        out_shape=jax.ShapeDtypeStruct((LANES // 2, 2 * half), F32),
        name="unpack",
    )(packed)


def per_device(n_anc, anchors, candidates, anchor_group, cand_group, cotangent):
    n, width = anchors.shape
    n_cand = NX * NY
    share = n // n_cand
    anc, cand = lax.axis_index("anc"), lax.axis_index("cand")
    core = anc % 2
    y, x = cand // NX, cand % NX

    def swap(v, over_x):
        pairs = []
        for p in range(n_anc):
            for j in range(NY):
                for i in range(NX):
                    k = i if over_x else j
                    k += 1 if (k - p) % 2 == 0 else -1
                    to = j * NX + k % NX if over_x else (k % NY) * NX + i
                    pairs.append((p * n_cand + j * NX + i, p * n_cand + to))
        return lax.ppermute(v, ("anc", "cand"), pairs)

    ag, cg = anchor_group.reshape(1, n), cand_group.reshape(-1, 1)
    an, cn, expo, st, ir = score_stage(anchors, candidates, ag, cg, n_cand)
    st = lax.all_to_all(st, "cand", 0, 0, tiled=True)
    cost, coef, own, oth = candidate_stage(
        core.reshape(1).astype(jnp.int32), st, cotangent.reshape(1, n), ag, cg, expo, an,
        candidates, ir,
    )

    sibling = lax.ppermute(oth, "anc", [(p, p ^ 1) for p in range(n_anc)])
    packed = lax.psum_scatter(
        own + sibling, "anc", scatter_dimension=0,
        axis_index_groups=[list(range(c, n_anc, 2)) for c in range(2)], tiled=False,
    )
    grad_candidates = unpack_stage(packed).T

    at = jnp.stack([x % 2, y % 2]).astype(jnp.int32)
    xkeep, xsend, ykeep, ysend = anchor_stage(at, coef.reshape(-1, n), cn, share)
    xgot, ygot = swap(xsend, True), swap(ysend, False)
    xagain, yagain = swap(xkeep[1] + xgot[1], False), swap(ykeep[1] + ygot[1], True)
    xpart, ypart = xkeep[0] + xgot[0] + xagain, ykeep[0] + ygot[0] + yagain
    groups = [
        [(2 * p + j) * NX + 2 * q + i for p in range(NY // 2) for q in range(NX // 2)]
        for j in range(2) for i in range(2)
    ]
    terms = jnp.concatenate([xpart, ypart], axis=-1).reshape(-1, share, width)
    terms = lax.all_to_all(terms, "cand", 0, 0, axis_index_groups=groups, tiled=True)
    rows = lax.dynamic_slice_in_dim(anchors, cand * share, share, 0)
    probe_derivatives = probe_stage(terms, rows)
    return cost.reshape(n), probe_derivatives, grad_candidates


def solution(mesh):
    in_specs = (P("anc", None), P("cand", None), P("anc"), P("cand"), P("anc"))
    out_specs = (P("anc"), P(("anc", "cand"), None), P("cand", "anc"))
    return jax.shard_map(
        functools.partial(per_device, mesh.shape["anc"]),
        mesh=mesh, in_specs=in_specs, out_specs=out_specs, check_vma=False,
    )
```

```python
import functools

import jax
import jax.numpy as jnp
from jax import lax
from jax.experimental import pallas as pl
from jax.experimental.pallas import tpu as pltpu
from jax.sharding import PartitionSpec as P

SCALE = 20.0
EPS = 1e-06
F32 = jnp.float32
BF16 = jnp.bfloat16
NX, NY = 4, 8
LANES = 128
SLOTS = 12
MIB = 2**20
VMEM = pl.BlockSpec(memory_space=pltpu.VMEM)
HBM = pl.BlockSpec(memory_space=pltpu.HBM)
SMEM = pl.BlockSpec(memory_space=pltpu.SMEM)


def inverse_radius(values):
    return 1.0 / jnp.sqrt(jnp.sum(values * values, axis=1, keepdims=True) + EPS)


class Copies:
    def __init__(self, sems):
        self.sems, self.all = sems, []

    def start(self, source, target):
        copy = pltpu.make_async_copy(source, target, self.sems.at[len(self.all)])
        copy.start()
        self.all.append(copy)
        return copy


SCORE_STEPS = 4
SCORE_COPIES = 3 + 4 * SCORE_STEPS


def score_kernel(
    a_hbm, c_hbm, ag_ref, cg_ref, an_hbm, cn_hbm, e_hbm, st_hbm, row_hbm,
    a_ref, c_ref, an_ref, cn_ref, e_ref, st_ref, row_ref, acc_ref, sems,
):
    n, m = a_ref.shape[0], c_ref.shape[0]
    per = n // LANES
    rows = m // SCORE_STEPS
    parts = [pl.ds(k * rows, rows) for k in range(SCORE_STEPS)]
    copies = Copies(sems)
    a_copy = copies.start(a_hbm, a_ref)
    c_copies = [copies.start(c_hbm.at[part], c_ref.at[part]) for part in parts]
    out = []
    for k in range(0, m, LANES):
        size = min(LANES, m - k)
        row_ref[k : k + size, :] = jnp.broadcast_to(
            cg_ref[:, k : k + size].astype(F32), (LANES, size)
        ).T
    a_copy.wait()
    for r in range(0, n, LANES):
        values = a_ref[r : r + LANES, :].astype(F32)
        an_ref[r : r + LANES, :] = (values * inverse_radius(values)).astype(BF16)
    out.append(copies.start(an_ref, an_hbm))
    ag = ag_ref[...].astype(F32)
    left = lax.broadcasted_iota(jnp.int32, (rows, LANES), 1) < LANES // 2
    acc = None
    for part, c_copy in zip(parts, c_copies):
        c_copy.wait()
        values = c_ref[part, :].astype(F32)
        inv = inverse_radius(values)
        cn = (values * inv).astype(BF16)
        cn_ref[part, :] = cn
        out.append(copies.start(cn_ref.at[part], cn_hbm.at[part]))
        scores = SCALE * lax.dot_general(
            cn, an_ref[...], (((1,), (1,)), ((), ())), preferred_element_type=F32
        )
        expo = jnp.exp(scores - SCALE)
        e_ref[part, :] = expo
        out.append(copies.start(e_ref.at[part], e_hbm.at[part]))
        group = row_ref[part, :]
        row_ref[part, :] = jnp.where(left, inv, group)
        out.append(copies.start(row_ref.at[part], row_hbm.at[part]))
        match = group[:, LANES - 1 :] == ag
        sums = (
            jnp.sum(expo, axis=0, keepdims=True),
            jnp.sum(jnp.where(match, 1.0, 0.0), axis=0, keepdims=True),
            jnp.sum(jnp.where(match, scores, 0.0), axis=0, keepdims=True),
        )
        acc = sums if acc is None else tuple(u + v for u, v in zip(acc, sums))
    for k, s in enumerate(acc):
        for j in range(per):
            acc_ref[k * per + j : k * per + j + 1, :] = s[:, j * LANES : (j + 1) * LANES]
    st_ref[...] = jnp.broadcast_to(acc_ref[...][None], st_ref.shape)
    out.append(copies.start(st_ref, st_hbm))
    for copy in out:
        copy.wait()


def score_stage(anchors, candidates, ag, cg, copies):
    n, width = anchors.shape
    m = candidates.shape[0]
    shapes = [
        ((n, width), BF16),
        ((m, width), BF16),
        ((m, n), F32),
        ((copies, SLOTS, LANES), F32),
        ((m, LANES), F32),
    ]
    return pl.pallas_call(
        score_kernel,
        in_specs=[HBM, HBM, VMEM, VMEM],
        out_specs=[HBM] * 5,
        out_shape=[jax.ShapeDtypeStruct(*s) for s in shapes],
        scratch_shapes=[
            pltpu.VMEM((n, width), BF16),
            pltpu.VMEM((m, width), BF16),
            *(pltpu.VMEM(*s) for s in shapes),
            pltpu.VMEM((SLOTS, LANES), F32),
            pltpu.SemaphoreType.DMA((SCORE_COPIES,)),
        ],
        compiler_params=pltpu.CompilerParams(vmem_limit_bytes=62 * MIB),
        name="scores",
    )(anchors, candidates, ag, cg)


CANDIDATE_STEPS = 3
CANDIDATE_COPIES = 2 + 6 * CANDIDATE_STEPS


def candidate_kernel(
    at_ref, st_hbm, cot_ref, ag_ref, row_hbm, e_hbm, an_hbm, c_hbm,
    cost_ref, coef_hbm, own_hbm, oth_hbm,
    st_ref, row_ref, e_ref, an_ref, c_ref, coef_ref, own_ref, oth_ref, sems,
):
    n = ag_ref.shape[1]
    half = own_ref.shape[1]
    rows = half // CANDIDATE_STEPS
    per = n // LANES
    parts = [pl.ds(k * rows, rows) for k in range(CANDIDATE_STEPS)]
    copies = Copies(sems)
    st_copy = copies.start(st_hbm, st_ref)
    ready = []
    for k, part in enumerate(parts):
        ready.append([
            copies.start(ref.at[:, part], to.at[:, part])
            for ref, to in ((row_hbm, row_ref), (e_hbm, e_ref), (c_hbm, c_ref))
        ])
        if k == 0:
            an_copy = copies.start(an_hbm, an_ref)
    out = []
    st_copy.wait()
    st = jnp.sum(st_ref[...], axis=0)
    total, count, positive = (
        jnp.concatenate([st[k * per + j : k * per + j + 1, :] for j in range(per)], axis=1)
        for k in range(3)
    )
    count = jnp.maximum(count, 1.0)
    cost_ref[...] = SCALE + jnp.log(total) - positive / count
    cot = cot_ref[...] * SCALE
    per_total, per_count = 1.0 / total, 1.0 / count
    ag = ag_ref[...].astype(F32)
    low = lax.broadcasted_iota(jnp.int32, (rows, LANES), 1) < LANES // 2
    first = at_ref[2] == 0

    def coefficients(side, part):
        match = row_ref[side, part, LANES - 1 :] == ag
        coef = (cot * (e_ref[side, part, :] * per_total - jnp.where(match, per_count, 0.0))).astype(BF16)
        coef_ref[side, part, :] = coef
        return coef

    def terms(side, part, coef):
        dcn = jnp.dot(coef, an_ref[...], preferred_element_type=F32)
        values = c_ref[side, part, :].astype(F32)
        inv = row_ref[side, part, :1]
        inner = jnp.sum(values * dcn, axis=1, keepdims=True)
        return inv * (dcn - values * (inv * inv * inner))

    for k, part in enumerate(parts):
        for copy in ready[k]:
            copy.wait()
        coefs = [coefficients(side, part) for side in range(2)]
        out.append(copies.start(coef_ref.at[:, part], coef_hbm.at[:, part]))
        if k == 0:
            an_copy.wait()
        over, under = (terms(side, part, coefs[side]) for side in range(2))
        for z in range(own_ref.shape[0]):
            top = over[:, z * LANES : (z + 1) * LANES]
            bottom = under[:, z * LANES : (z + 1) * LANES]
            even = jnp.where(low, top, pltpu.roll(bottom, LANES // 2, 1))
            odd = jnp.where(low, pltpu.roll(top, LANES // 2, 1), bottom)
            own_ref[z, part, :] = jnp.where(first, even, odd)
            oth_ref[z, part, :] = jnp.where(first, odd, even)
        out.append(copies.start(oth_ref.at[:, part], oth_hbm.at[:, part]))
        out.append(copies.start(own_ref.at[:, part], own_hbm.at[:, part]))
    for copy in out:
        copy.wait()


def candidate_stage(at, st, cot, ag, row, expo, an, candidates):
    n, width = an.shape
    half = candidates.shape[0] // 2
    ins = [
        (st.shape, F32),
        ((2, half, LANES), F32),
        ((2, half, n), F32),
        ((n, width), BF16),
        ((2, half, width), BF16),
    ]
    outs = [((2, half, n), BF16)] + [((width // LANES, half, LANES), F32)] * 2
    return pl.pallas_call(
        candidate_kernel,
        in_specs=[SMEM, HBM, VMEM, VMEM, HBM, HBM, HBM, HBM],
        out_specs=[VMEM, HBM, HBM, HBM],
        out_shape=[jax.ShapeDtypeStruct((1, n), F32)] + [jax.ShapeDtypeStruct(*s) for s in outs],
        scratch_shapes=[
            *(pltpu.VMEM(*s) for s in ins + outs),
            pltpu.SemaphoreType.DMA((CANDIDATE_COPIES,)),
        ],
        compiler_params=pltpu.CompilerParams(vmem_limit_bytes=61 * MIB),
        name="candidate_terms",
    )(
        at, st, cot, ag, row.reshape(ins[1][0]), expo.reshape(ins[2][0]), an,
        candidates.reshape(ins[4][0]),
    )


def anchor_kernel(at_ref, coef_hbm, cn_hbm, xkeep, xsend, ykeep, ysend, coef_ref, cn_ref, scr, sems):
    copies = Copies(sems)
    share, cols = xkeep.shape[3:]
    coef_copy = copies.start(coef_hbm, coef_ref)
    cn_copies = [
        copies.start(cn_hbm.at[:, pl.ds(h * cols, cols)], cn_ref.at[h]) for h in range(2)
    ]
    x0, y0 = at_ref[0], at_ref[1]

    def rows(p, y, q, x):
        place = (2 * p + y) * NX + 2 * q + x
        return pl.ds(pl.multiple_of(place * share, share), share)

    out = []
    coef_copy.wait()
    coef = coef_ref[...]
    for h, (keep, send) in enumerate(((xkeep, xsend), (ykeep, ysend))):
        cn_copies[h].wait()
        scr[h] = lax.dot_general(
            coef, cn_ref[h], (((0,), (0,)), ((), ())), preferred_element_type=F32
        )
        for other in range(2):
            for p in range(NY // 2):
                for q in range(NX // 2):
                    if h == 0:
                        y = y0 if other == 0 else 1 - y0
                        mine, theirs = rows(p, y, q, x0), rows(p, y, q, 1 - x0)
                    else:
                        x = x0 if other == 0 else 1 - x0
                        mine, theirs = rows(p, y0, q, x), rows(p, 1 - y0, q, x)
                    out.append(copies.start(scr.at[h, theirs], send.at[other, p, q]))
                    out.append(copies.start(scr.at[h, mine], keep.at[other, p, q]))
    for copy in out:
        copy.wait()


def anchor_stage(at, coef, cn, share):
    m, width = cn.shape
    n = coef.shape[1]
    cols = width // 2
    part = jax.ShapeDtypeStruct((2, NY // 2, NX // 2, share, cols), F32)
    return pl.pallas_call(
        anchor_kernel,
        in_specs=[SMEM, HBM, HBM],
        out_specs=[HBM] * 4,
        out_shape=[part] * 4,
        scratch_shapes=[
            pltpu.VMEM((m, n), BF16),
            pltpu.VMEM((2, m, cols), BF16),
            pltpu.VMEM((2, n, cols), F32),
            pltpu.SemaphoreType.DMA((3 + 2 * NX * NY,)),
        ],
        compiler_params=pltpu.CompilerParams(vmem_limit_bytes=60 * MIB),
        cost_estimate=pl.CostEstimate(
            flops=2 * n * width * m, bytes_accessed=8 * MIB, transcendentals=0
        ),
        name="anchor_terms",
    )(at, coef, cn)


def probe_kernel(t_ref, a_ref, o_ref):
    term = jnp.sum(t_ref[...], axis=0)
    values = a_ref[...].astype(F32)
    inv = inverse_radius(values)
    unit = values * inv
    o_ref[...] = (term - unit * jnp.sum(unit * term, axis=1, keepdims=True)) * inv


def probe_stage(terms, rows):
    return pl.pallas_call(
        probe_kernel,
        out_shape=jax.ShapeDtypeStruct(rows.shape, F32),
        compiler_params=pltpu.CompilerParams(vmem_limit_bytes=8 * MIB),
        name="probe_derivatives",
    )(terms, rows)


def unpack_kernel(p_ref, o_ref):
    half = p_ref.shape[0]
    t = p_ref[...].T
    o_ref[:, :half] = t[: LANES // 2]
    o_ref[:, half:] = t[LANES // 2 :]


def unpack_stage(packed):
    half = packed.shape[0]
    return pl.pallas_call(
        unpack_kernel,
        out_shape=jax.ShapeDtypeStruct((LANES // 2, 2 * half), F32),
        compiler_params=pltpu.CompilerParams(vmem_limit_bytes=62 * MIB),
        name="unpack",
    )(packed)


def per_device(n_anc, anchors, candidates, anchor_group, cand_group, cotangent):
    n, width = anchors.shape
    n_cand = NX * NY
    share = n // n_cand
    anc, cand = lax.axis_index("anc"), lax.axis_index("cand")
    core = anc % 2
    y, x = cand // NX, cand % NX

    def swap(v, over_x):
        pairs = []
        for p in range(n_anc):
            for j in range(NY):
                for i in range(NX):
                    k = i if over_x else j
                    k += 1 if (k - p) % 2 == 0 else -1
                    to = j * NX + k % NX if over_x else (k % NY) * NX + i
                    pairs.append((p * n_cand + j * NX + i, p * n_cand + to))
        return lax.ppermute(v, ("anc", "cand"), pairs)

    ag, cg = anchor_group.reshape(1, n), cand_group.reshape(1, -1)
    an, cn, expo, st, row = score_stage(anchors, candidates, ag, cg, n_cand)
    st = lax.all_to_all(st, "cand", 0, 0, tiled=True)
    at = jnp.stack([x % 2, y % 2, core]).astype(jnp.int32)
    cost, coef, own, oth = candidate_stage(
        at, st, cotangent.reshape(1, n), ag, row, expo, an,
        candidates,
    )

    sibling = lax.ppermute(oth, "anc", [(p, p ^ 1) for p in range(n_anc)])
    parts = anchor_stage(at, coef.reshape(-1, n), cn, share)
    own, parts = lax.optimization_barrier((own, parts))
    both, parts = lax.optimization_barrier((own + sibling, parts))
    packed = lax.psum_scatter(
        both, "anc", scatter_dimension=0,
        axis_index_groups=[list(range(c, n_anc, 2)) for c in range(2)], tiled=False,
    )
    grad_candidates = unpack_stage(packed).T

    xkeep, xsend, ykeep, ysend = parts
    xgot, ygot = swap(xsend, True), swap(ysend, False)
    xagain, yagain = swap(xkeep[1] + xgot[1], False), swap(ykeep[1] + ygot[1], True)
    xpart, ypart = xkeep[0] + xgot[0] + xagain, ykeep[0] + ygot[0] + yagain
    groups = [
        [(2 * p + j) * NX + 2 * q + i for p in range(NY // 2) for q in range(NX // 2)]
        for j in range(2) for i in range(2)
    ]
    terms = jnp.concatenate([xpart, ypart], axis=-1).reshape(-1, share, width)
    terms = lax.all_to_all(terms, "cand", 0, 0, axis_index_groups=groups, tiled=True)
    rows = lax.dynamic_slice_in_dim(anchors, cand * share, share, 0)
    probe_derivatives = probe_stage(terms, rows)
    return cost.reshape(n), probe_derivatives, grad_candidates


def solution(mesh):
    in_specs = (P("anc", None), P("cand", None), P("anc"), P("cand"), P("anc"))
    out_specs = (P("anc"), P(("anc", "cand"), None), P("cand", "anc"))
    return jax.shard_map(
        functools.partial(per_device, mesh.shape["anc"]),
        mesh=mesh, in_specs=in_specs, out_specs=out_specs, check_vma=False,
    )
```

```python
import functools

import jax
import jax.numpy as jnp
from jax import lax
from jax.experimental import pallas as pl
from jax.experimental.pallas import tpu as pltpu
from jax.sharding import PartitionSpec as P

SCALE = 20.0
EPS = 1e-06
F32 = jnp.float32
BF16 = jnp.bfloat16
NX, NY = 4, 8
LANES = 128
SLOTS = 12
SPARE = 8
MIB = 2**20
VMEM = pl.BlockSpec(memory_space=pltpu.VMEM)
HBM = pl.BlockSpec(memory_space=pltpu.HBM)
SMEM = pl.BlockSpec(memory_space=pltpu.SMEM)


def inverse_radius(values):
    return 1.0 / jnp.sqrt(jnp.sum(values * values, axis=1, keepdims=True) + EPS)


class Copies:
    def __init__(self, sems):
        self.sems, self.all = sems, []

    def start(self, source, target):
        copy = pltpu.make_async_copy(source, target, self.sems.at[len(self.all)])
        copy.start()
        self.all.append(copy)
        return copy


def core_columns(values, core):
    side = (lax.broadcasted_iota(jnp.int32, (values.shape[0], LANES), 1) >= LANES // 2).astype(jnp.int32)
    stay = side == core
    blocks = []
    for k in range(0, values.shape[1], 2 * LANES):
        left, right = values[:, k : k + LANES], values[:, k + LANES : k + 2 * LANES]
        kept = jnp.where(core == 0, left, right)
        moved = jnp.where(core == 0, right, left)
        blocks.append(jnp.where(stay, kept, pltpu.roll(moved, LANES // 2, 1)))
    return blocks


SCORE_STEPS = 4
SCORE_COPIES = 4 + 4 * SCORE_STEPS


def score_kernel(
    a_hbm, c_hbm, ag_ref, cg_ref, cot_ref, an_hbm, x_hbm, st_hbm, row_hbm, cc_hbm,
    a_ref, c_ref, full_ref, an_ref, x_ref, st_ref, row_ref, cc_ref, acc_ref, sems,
):
    n, m = a_ref.shape[0], c_ref.shape[0]
    per = n // LANES
    core = lax.axis_index("anc") % 2
    rows = m // SCORE_STEPS
    parts = [pl.ds(k * rows, rows) for k in range(SCORE_STEPS)]
    copies = Copies(sems)
    a_copy = copies.start(a_hbm, a_ref)
    c_copies = [copies.start(c_hbm.at[part], c_ref.at[part]) for part in parts]
    out = []
    for k in range(0, m, LANES):
        size = min(LANES, m - k)
        row_ref[k : k + size, :] = jnp.broadcast_to(
            cg_ref[:, k : k + size].astype(F32), (LANES, size)
        ).T
    ag = ag_ref[...].astype(F32)
    x_ref[m + n : m + n + SPARE, :] = jnp.zeros((SPARE, n), F32)
    x_ref[m + n : m + n + 1, :] = ag
    x_ref[m + n + 1 : m + n + 2, :] = cot_ref[...]
    a_copy.wait()
    for r in range(0, n, LANES):
        values = a_ref[r : r + LANES, :].astype(F32)
        unit = values * inverse_radius(values)
        full_ref[r : r + LANES, :] = unit.astype(BF16)
        for k, block in enumerate(core_columns(unit, core)):
            an_ref[r : r + LANES, k * LANES : (k + 1) * LANES] = block.astype(BF16)
        for k, block in enumerate(core_columns(unit, 1 - core)):
            first = m + r if k < per else m + n + SPARE + r
            k = k % per
            x_ref[first : first + LANES, k * LANES : (k + 1) * LANES] = block
    rest = pl.ds(m, x_ref.shape[0] - m)
    out.append(copies.start(x_ref.at[rest], x_hbm.at[rest]))
    out.append(copies.start(an_ref, an_hbm))
    left = lax.broadcasted_iota(jnp.int32, (rows, LANES), 1) < LANES // 2
    acc = None
    for part, c_copy in zip(parts, c_copies):
        c_copy.wait()
        values = c_ref[part, :].astype(F32)
        inv = inverse_radius(values)
        scores = SCALE * lax.dot_general(
            (values * inv).astype(BF16), full_ref[...], (((1,), (1,)), ((), ())),
            preferred_element_type=F32,
        )
        expo = jnp.exp(scores - SCALE)
        x_ref[part, :] = expo
        out.append(copies.start(x_ref.at[part], x_hbm.at[part]))
        group = row_ref[part, :]
        row_ref[part, :] = jnp.where(left, inv, group)
        out.append(copies.start(row_ref.at[part], row_hbm.at[part]))
        for k, block in enumerate(core_columns(values, core)):
            cc_ref[part, k * LANES : (k + 1) * LANES] = block.astype(BF16)
        out.append(copies.start(cc_ref.at[part], cc_hbm.at[part]))
        match = group[:, LANES - 1 :] == ag
        sums = (
            jnp.sum(expo, axis=0, keepdims=True),
            jnp.sum(jnp.where(match, 1.0, 0.0), axis=0, keepdims=True),
            jnp.sum(jnp.where(match, scores, 0.0), axis=0, keepdims=True),
        )
        acc = sums if acc is None else tuple(u + v for u, v in zip(acc, sums))
    for k, s in enumerate(acc):
        for j in range(per):
            acc_ref[k * per + j : k * per + j + 1, :] = s[:, j * LANES : (j + 1) * LANES]
    st_ref[...] = jnp.broadcast_to(acc_ref[...][None], st_ref.shape)
    out.append(copies.start(st_ref, st_hbm))
    for copy in out:
        copy.wait()


def score_stage(anchors, candidates, ag, cg, cot, copies):
    n, width = anchors.shape
    m = candidates.shape[0]
    shapes = [
        ((n, width // 2), BF16),
        ((m + 2 * n + SPARE, n), F32),
        ((copies, SLOTS, LANES), F32),
        ((m, LANES), F32),
        ((m, width // 2), BF16),
    ]
    return pl.pallas_call(
        score_kernel,
        in_specs=[HBM, HBM, VMEM, VMEM, VMEM],
        out_specs=[HBM] * 5,
        out_shape=[jax.ShapeDtypeStruct(*s) for s in shapes],
        scratch_shapes=[
            pltpu.VMEM((n, width), BF16),
            pltpu.VMEM((m, width), BF16),
            pltpu.VMEM((n, width), BF16),
            *(pltpu.VMEM(*s) for s in shapes),
            pltpu.VMEM((SLOTS, LANES), F32),
            pltpu.SemaphoreType.DMA((SCORE_COPIES,)),
        ],
        compiler_params=pltpu.CompilerParams(vmem_limit_bytes=62 * MIB),
        name="scores",
    )(anchors, candidates, ag, cg, cot)


CANDIDATE_STEPS = 3
CANDIDATE_COPIES = 3 + 6 * CANDIDATE_STEPS


def candidate_kernel(
    st_ref, other_ref, cot_ref, ag_ref, row_hbm, cc_hbm, an_hbm, x_hbm, y_hbm,
    cost_ref, coef_hbm, own_hbm,
    row_ref, cc_ref, x_ref, y_ref, an_ref, extra_ref, more_ref, coef_ref, own_ref, sems,
):
    n = ag_ref.shape[1]
    half = own_ref.shape[1]
    m = 2 * half
    rows = half // CANDIDATE_STEPS
    per = n // LANES
    wide = more_ref.shape[1]
    parts = [pl.ds(k * rows, rows) for k in range(CANDIDATE_STEPS)]
    copies = Copies(sems)
    extra_copy = copies.start(y_hbm.at[pl.ds(m, n + SPARE)], extra_ref)
    more_copy = copies.start(
        y_hbm.at[pl.ds(m + n + SPARE, n), pl.ds(0, wide)], more_ref
    )
    an_copy = copies.start(an_hbm, an_ref.at[pl.ds(0, n)])
    ready = []
    for part in parts:
        ready.append([copies.start(row_hbm.at[:, part], row_ref.at[:, part])])
        for side in range(2):
            place = pl.ds(side * half + part.start, rows)
            ready[-1].append(copies.start(x_hbm.at[place], x_ref.at[side, part]))
            ready[-1].append(copies.start(y_hbm.at[place], y_ref.at[side, part]))
        ready[-1].append(copies.start(cc_hbm.at[:, part], cc_ref.at[:, part]))
    out = []

    def sums(ref):
        st = ref[...]
        total, count, positive = (
            jnp.concatenate([st[k * per + j : k * per + j + 1, :] for j in range(per)], axis=1)
            for k in range(3)
        )
        return total, jnp.maximum(count, 1.0), positive

    total, count, positive = sums(st_ref)
    cost_ref[...] = SCALE + jnp.log(total) - positive / count
    extra_copy.wait()
    factors = [(SCALE * cot_ref[...], 1.0 / total, 1.0 / count, ag_ref[...].astype(F32))]
    total, count, _ = sums(other_ref)
    factors.append((SCALE * extra_ref[n + 1 : n + 2, :], 1.0 / total, 1.0 / count, extra_ref[n : n + 1, :]))
    an_ref[n:, :n] = extra_ref[:n, :].astype(BF16)
    more_copy.wait()
    an_ref[n:, n:] = more_ref[...].astype(BF16)
    low = lax.broadcasted_iota(jnp.int32, (rows, LANES), 1) < LANES // 2

    def coefficients(ref, side, part, factor):
        cot, per_total, per_count, ag = factor
        match = row_ref[side, part, LANES - 1 :] == ag
        expo = ref[side, part, :]
        coef = (cot * (expo * per_total - jnp.where(match, per_count, 0.0))).astype(BF16)
        cosine = 1.0 + jnp.log(expo) * (1.0 / SCALE)
        return coef, jnp.sum(coef.astype(F32) * cosine, axis=1, keepdims=True)

    for k, part in enumerate(parts):
        for copy in ready[k]:
            copy.wait()
        coefs = []
        for side in range(2):
            mine, inner = coefficients(x_ref, side, part, factors[0])
            theirs, more = coefficients(y_ref, side, part, factors[1])
            coef_ref[side, part, :] = mine
            coefs.append((jnp.concatenate([mine, theirs], axis=1), inner + more))
        out.append(copies.start(coef_ref.at[:, part], coef_hbm.at[:, part]))
        if k == 0:
            an_copy.wait()
        grads = []
        for side, (coef, inner) in enumerate(coefs):
            dcn = jnp.dot(coef, an_ref[...], preferred_element_type=F32)
            inv = row_ref[side, part, :1]
            grads.append(inv * (dcn - cc_ref[side, part, :].astype(F32) * (inv * inner)))
        over, under = grads
        for b in range(own_ref.shape[0] // 2):
            top = over[:, b * LANES : (b + 1) * LANES]
            bottom = under[:, b * LANES : (b + 1) * LANES]
            own_ref[2 * b, part, :] = jnp.where(low, top, pltpu.roll(bottom, LANES // 2, 1))
            own_ref[2 * b + 1, part, :] = jnp.where(low, pltpu.roll(top, LANES // 2, 1), bottom)
        out.append(copies.start(own_ref.at[:, part], own_hbm.at[:, part]))
    for copy in out:
        copy.wait()


def candidate_stage(st, other, cot, ag, row, cc, an, x, y):
    n, cols = an.shape
    half = row.shape[0] // 2
    split = lambda v: v.reshape(2, half, -1)
    outs = [((2, half, n), BF16), ((2 * cols // LANES, half, LANES), F32)]
    scratch = [
        ((2, half, LANES), F32),
        ((2, half, cols), BF16),
        ((2, half, n), F32),
        ((2, half, n), F32),
        ((2 * n, cols), BF16),
        ((n + SPARE, n), F32),
        ((n, cols - n), F32),
    ]
    return pl.pallas_call(
        candidate_kernel,
        in_specs=[VMEM] * 4 + [HBM] * 5,
        out_specs=[VMEM, HBM, HBM],
        out_shape=[jax.ShapeDtypeStruct(*s) for s in [((1, n), F32)] + outs],
        scratch_shapes=[
            *(pltpu.VMEM(*s) for s in scratch + outs),
            pltpu.SemaphoreType.DMA((CANDIDATE_COPIES + 2 * CANDIDATE_STEPS,)),
        ],
        compiler_params=pltpu.CompilerParams(vmem_limit_bytes=60 * MIB),
        name="candidate_terms",
    )(st, other, cot, ag, split(row), split(cc), an, x, y)


def anchor_kernel(
    coef_hbm, row_hbm, c_hbm, xkeep, xsend, ykeep, ysend, coef_ref, row_ref, c_ref, scr, sems,
):
    copies = Copies(sems)
    share, cols = xkeep.shape[3:]
    row_copy = copies.start(row_hbm, row_ref)
    c_copies = [copies.start(c_hbm.at[:, pl.ds(h * cols, cols)], c_ref.at[h]) for h in range(2)]
    coef_copy = copies.start(coef_hbm, coef_ref)
    cand = lax.axis_index("cand")
    x0, y0 = cand % 2, (cand // NX) % 2

    out = []
    row_copy.wait()
    inv = row_ref[:, :1]
    for h, (keep, send) in enumerate(((xkeep, xsend), (ykeep, ysend))):
        c_copies[h].wait()
        cn = (c_ref[h].astype(F32) * inv).astype(BF16)
        if h == 0:
            coef_copy.wait()
        scr[h] = lax.dot_general(
            coef_ref[...], cn, (((0,), (0,)), ((), ())), preferred_element_type=F32
        ).reshape(scr.shape[1:])
        for other in range(2):
            if h == 0:
                y = y0 if other == 0 else 1 - y0
                mine, theirs = (y, x0), (y, 1 - x0)
            else:
                x = x0 if other == 0 else 1 - x0
                mine, theirs = (y0, x), (1 - y0, x)
            for (j, i), to in ((theirs, send), (mine, keep)):
                out.append(copies.start(scr.at[h, :, j, :, i], to.at[other]))
    for copy in out:
        copy.wait()


def anchor_stage(coef, row, candidates, share):
    m, width = candidates.shape
    n = coef.shape[1]
    cols = width // 2
    part = jax.ShapeDtypeStruct((2, NY // 2, NX // 2, share, cols), F32)
    return pl.pallas_call(
        anchor_kernel,
        in_specs=[HBM, HBM, HBM],
        out_specs=[HBM] * 4,
        out_shape=[part] * 4,
        scratch_shapes=[
            pltpu.VMEM((m, n), BF16),
            pltpu.VMEM((m, LANES), F32),
            pltpu.VMEM((2, m, cols), BF16),
            pltpu.VMEM((2, NY // 2, 2, NX // 2, 2, share, cols), F32),
            pltpu.SemaphoreType.DMA((12,)),
        ],
        compiler_params=pltpu.CompilerParams(vmem_limit_bytes=60 * MIB),
        cost_estimate=pl.CostEstimate(
            flops=2 * n * width * m, bytes_accessed=8 * MIB, transcendentals=0
        ),
        name="anchor_terms",
    )(coef, row, candidates)


def probe_kernel(t_ref, a_ref, o_ref):
    term = jnp.sum(t_ref[...], axis=0)
    values = a_ref[...].astype(F32)
    inv = inverse_radius(values)
    unit = values * inv
    o_ref[...] = (term - unit * jnp.sum(unit * term, axis=1, keepdims=True)) * inv


def probe_stage(terms, rows):
    return pl.pallas_call(
        probe_kernel,
        out_shape=jax.ShapeDtypeStruct(rows.shape, F32),
        compiler_params=pltpu.CompilerParams(vmem_limit_bytes=8 * MIB),
        name="probe_derivatives",
    )(terms, rows)


def unpack_kernel(p_ref, o_ref):
    half = p_ref.shape[0]
    t = p_ref[...].T
    o_ref[:, :half] = t[: LANES // 2]
    o_ref[:, half:] = t[LANES // 2 :]


def unpack_stage(packed):
    half = packed.shape[0]
    return pl.pallas_call(
        unpack_kernel,
        out_shape=jax.ShapeDtypeStruct((LANES // 2, 2 * half), F32),
        compiler_params=pltpu.CompilerParams(vmem_limit_bytes=62 * MIB),
        name="unpack",
    )(packed)


def per_device(n_anc, anchors, candidates, anchor_group, cand_group, cotangent):
    n, width = anchors.shape
    n_cand = NX * NY
    share = n // n_cand
    cand = lax.axis_index("cand")

    def swap(v, over_x):
        pairs = []
        for p in range(n_anc):
            for j in range(NY):
                for i in range(NX):
                    k = i if over_x else j
                    k += 1 if (k - p) % 2 == 0 else -1
                    to = j * NX + k % NX if over_x else (k % NY) * NX + i
                    pairs.append((p * n_cand + j * NX + i, p * n_cand + to))
        return lax.ppermute(v, ("anc", "cand"), pairs)

    def sibling(v):
        return lax.ppermute(v, "anc", [(p, p ^ 1) for p in range(n_anc)])

    ag, cg, cot = anchor_group.reshape(1, n), cand_group.reshape(1, -1), cotangent.reshape(1, n)
    an, mine, st, row, cc = score_stage(anchors, candidates, ag, cg, cot, n_cand)

    theirs = sibling(mine)
    st = jnp.sum(lax.all_to_all(st, "cand", 0, 0, tiled=True), axis=0)
    cost, coef, packed = candidate_stage(st, sibling(st), cot, ag, row, cc, an, mine, theirs)
    packed = lax.psum_scatter(
        packed, "anc", scatter_dimension=0,
        axis_index_groups=[list(range(c, n_anc, 2)) for c in range(2)], tiled=False,
    )
    grad_candidates = unpack_stage(packed).T

    xkeep, xsend, ykeep, ysend = anchor_stage(coef.reshape(-1, n), row, candidates, share)
    xgot, ygot = swap(xsend, True), swap(ysend, False)
    xagain, yagain = swap(xkeep[1] + xgot[1], False), swap(ykeep[1] + ygot[1], True)
    xpart, ypart = xkeep[0] + xgot[0] + xagain, ykeep[0] + ygot[0] + yagain
    groups = [
        [(2 * p + j) * NX + 2 * q + i for p in range(NY // 2) for q in range(NX // 2)]
        for j in range(2) for i in range(2)
    ]
    terms = jnp.concatenate([xpart, ypart], axis=-1).reshape(-1, share, width)
    terms = lax.all_to_all(terms, "cand", 0, 0, axis_index_groups=groups, tiled=True)
    rows = lax.dynamic_slice_in_dim(anchors, cand * share, share, 0)
    probe_derivatives = probe_stage(terms, rows)
    return cost.reshape(n), probe_derivatives, grad_candidates


def solution(mesh):
    in_specs = (P("anc", None), P("cand", None), P("anc"), P("cand"), P("anc"))
    out_specs = (P("anc"), P(("anc", "cand"), None), P("cand", "anc"))
    return jax.shard_map(
        functools.partial(per_device, mesh.shape["anc"]),
        mesh=mesh, in_specs=in_specs, out_specs=out_specs, check_vma=False,
    )
```

```python
import functools

import jax
import jax.numpy as jnp
from jax import lax
from jax.experimental import pallas as pl
from jax.experimental.pallas import tpu as pltpu
from jax.sharding import PartitionSpec as P

SCALE = 20.0
EPS = 1e-06
F32 = jnp.float32
BF16 = jnp.bfloat16
NX, NY = 4, 8
LANES = 128
SLOTS = 12
SPARE = 8
MIB = 2**20
VMEM = pl.BlockSpec(memory_space=pltpu.VMEM)
HBM = pl.BlockSpec(memory_space=pltpu.HBM)
SMEM = pl.BlockSpec(memory_space=pltpu.SMEM)


def inverse_radius(values):
    return 1.0 / jnp.sqrt(jnp.sum(values * values, axis=1, keepdims=True) + EPS)


class Copies:
    def __init__(self, sems):
        self.sems, self.all = sems, []

    def start(self, source, target):
        copy = pltpu.make_async_copy(source, target, self.sems.at[len(self.all)])
        copy.start()
        self.all.append(copy)
        return copy


def core_columns(values, core):
    side = (lax.broadcasted_iota(jnp.int32, (values.shape[0], LANES), 1) >= LANES // 2).astype(jnp.int32)
    stay = side == core
    blocks = []
    for k in range(0, values.shape[1], 2 * LANES):
        left, right = values[:, k : k + LANES], values[:, k + LANES : k + 2 * LANES]
        kept = jnp.where(core == 0, left, right)
        moved = jnp.where(core == 0, right, left)
        blocks.append(jnp.where(stay, kept, pltpu.roll(moved, LANES // 2, 1)))
    return blocks


SCORE_STEPS = 4
SCORE_COPIES = 3 + 4 * SCORE_STEPS


def score_kernel(
    a_hbm, c_hbm, ag_ref, cg_ref, cot_ref, an_hbm, x_hbm, st_hbm, row_hbm, cc_hbm,
    a_ref, c_ref, full_ref, an_ref, x_ref, st_ref, row_ref, cc_ref, acc_ref, sems,
):
    n, m = a_ref.shape[0], c_ref.shape[0]
    per = n // LANES
    core = lax.axis_index("anc") % 2
    rows = m // SCORE_STEPS
    parts = [pl.ds(k * rows, rows) for k in range(SCORE_STEPS)]
    copies = Copies(sems)
    a_parts = [pl.ds(r, LANES) for r in range(0, n, LANES)]
    a_copies = [copies.start(a_hbm.at[part], a_ref.at[part]) for part in a_parts]
    c_copies = [copies.start(c_hbm.at[part], c_ref.at[part]) for part in parts]
    out = []
    for k in range(0, m, LANES):
        size = min(LANES, m - k)
        row_ref[k : k + size, :] = jnp.broadcast_to(
            cg_ref[:, k : k + size].astype(F32), (LANES, size)
        ).T
    ag = ag_ref[...].astype(F32)
    x_ref[m + n : m + n + SPARE, :] = jnp.zeros((SPARE, n), F32)
    x_ref[m + n : m + n + 1, :] = ag
    x_ref[m + n + 1 : m + n + 2, :] = cot_ref[...]
    for r, a_copy in zip(range(0, n, LANES), a_copies):
        a_copy.wait()
        values = a_ref[r : r + LANES, :].astype(F32)
        unit = values * inverse_radius(values)
        full_ref[r : r + LANES, :] = unit.astype(BF16)
        for k, block in enumerate(core_columns(unit, core)):
            an_ref[r : r + LANES, k * LANES : (k + 1) * LANES] = block.astype(BF16)
        for k, block in enumerate(core_columns(unit, 1 - core)):
            first = m + r if k < per else m + n + SPARE + r
            k = k % per
            x_ref[first : first + LANES, k * LANES : (k + 1) * LANES] = block
    rest = pl.ds(m, x_ref.shape[0] - m)
    out.append(copies.start(x_ref.at[rest], x_hbm.at[rest]))
    out.append(copies.start(an_ref, an_hbm))
    left = lax.broadcasted_iota(jnp.int32, (rows, LANES), 1) < LANES // 2
    acc = None
    for part, c_copy in zip(parts, c_copies):
        c_copy.wait()
        values = c_ref[part, :].astype(F32)
        inv = inverse_radius(values)
        scores = SCALE * lax.dot_general(
            (values * inv).astype(BF16), full_ref[...], (((1,), (1,)), ((), ())),
            preferred_element_type=F32,
        )
        expo = jnp.exp(scores - SCALE)
        x_ref[part, :] = expo
        out.append(copies.start(x_ref.at[part], x_hbm.at[part]))
        group = row_ref[part, :]
        row_ref[part, :] = jnp.where(left, inv, group)
        out.append(copies.start(row_ref.at[part], row_hbm.at[part]))
        for k, block in enumerate(core_columns(values, core)):
            cc_ref[part, k * LANES : (k + 1) * LANES] = block.astype(BF16)
        out.append(copies.start(cc_ref.at[part], cc_hbm.at[part]))
        match = group[:, LANES - 1 :] == ag
        sums = (
            jnp.sum(expo, axis=0, keepdims=True),
            jnp.sum(jnp.where(match, 1.0, 0.0), axis=0, keepdims=True),
            jnp.sum(jnp.where(match, scores, 0.0), axis=0, keepdims=True),
        )
        acc = sums if acc is None else tuple(u + v for u, v in zip(acc, sums))
    for k, s in enumerate(acc):
        for j in range(per):
            acc_ref[k * per + j : k * per + j + 1, :] = s[:, j * LANES : (j + 1) * LANES]
    st_ref[...] = jnp.broadcast_to(acc_ref[...][None], st_ref.shape)
    out.append(copies.start(st_ref, st_hbm))
    for copy in out:
        copy.wait()


def score_stage(anchors, candidates, ag, cg, cot, copies):
    n, width = anchors.shape
    m = candidates.shape[0]
    shapes = [
        ((n, width // 2), BF16),
        ((m + 2 * n + SPARE, n), F32),
        ((copies, SLOTS, LANES), F32),
        ((m, LANES), F32),
        ((m, width // 2), BF16),
    ]
    return pl.pallas_call(
        score_kernel,
        in_specs=[HBM, HBM, VMEM, VMEM, VMEM],
        out_specs=[HBM] * 5,
        out_shape=[jax.ShapeDtypeStruct(*s) for s in shapes],
        scratch_shapes=[
            pltpu.VMEM((n, width), BF16),
            pltpu.VMEM((m, width), BF16),
            pltpu.VMEM((n, width), BF16),
            *(pltpu.VMEM(*s) for s in shapes),
            pltpu.VMEM((SLOTS, LANES), F32),
            pltpu.SemaphoreType.DMA((SCORE_COPIES + n // LANES,)),
        ],
        compiler_params=pltpu.CompilerParams(vmem_limit_bytes=62 * MIB),
        name="scores",
    )(anchors, candidates, ag, cg, cot)


CANDIDATE_STEPS = 3
CANDIDATE_COPIES = 4 + 6 * CANDIDATE_STEPS


def candidate_kernel(
    st_ref, other_ref, cot_ref, ag_ref, row_hbm, cc_hbm, an_hbm, x_hbm, y_hbm,
    cost_ref, coef_hbm, own_hbm,
    row_ref, cc_ref, x_ref, y_ref, an_ref, extra_ref, more_ref, coef_ref, own_ref, sems,
):
    n = ag_ref.shape[1]
    half = own_ref.shape[1]
    m = 2 * half
    rows = half // CANDIDATE_STEPS
    per = n // LANES
    wide = more_ref.shape[1]
    parts = [pl.ds(k * rows, rows) for k in range(CANDIDATE_STEPS)]
    copies = Copies(sems)
    spare_copy = copies.start(y_hbm.at[pl.ds(m + n, SPARE)], extra_ref.at[pl.ds(n, SPARE)])
    ready, late = [], []
    for k, part in enumerate(parts):
        ready.append([copies.start(row_hbm.at[:, part], row_ref.at[:, part])])
        for side in range(2):
            place = pl.ds(side * half + part.start, rows)
            ready[k].append(copies.start(x_hbm.at[place], x_ref.at[side, part]))
            ready[k].append(copies.start(y_hbm.at[place], y_ref.at[side, part]))
        if k == 0:
            an_copy = copies.start(an_hbm, an_ref.at[pl.ds(0, n)])
            extra_copy = copies.start(y_hbm.at[pl.ds(m, n)], extra_ref.at[pl.ds(0, n)])
            more_copy = copies.start(y_hbm.at[pl.ds(m + n + SPARE, n), pl.ds(0, wide)], more_ref)
        late.append(copies.start(cc_hbm.at[:, part], cc_ref.at[:, part]))
    out = []

    def sums(ref):
        st = ref[...]
        total, count, positive = (
            jnp.concatenate([st[k * per + j : k * per + j + 1, :] for j in range(per)], axis=1)
            for k in range(3)
        )
        return total, jnp.maximum(count, 1.0), positive

    total, count, positive = sums(st_ref)
    cost_ref[...] = SCALE + jnp.log(total) - positive / count
    spare_copy.wait()
    factors = [(SCALE * cot_ref[...], 1.0 / total, 1.0 / count, ag_ref[...].astype(F32))]
    total, count, _ = sums(other_ref)
    factors.append((SCALE * extra_ref[n + 1 : n + 2, :], 1.0 / total, 1.0 / count, extra_ref[n : n + 1, :]))
    low = lax.broadcasted_iota(jnp.int32, (rows, LANES), 1) < LANES // 2

    def coefficients(ref, side, part, factor):
        cot, per_total, per_count, ag = factor
        match = row_ref[side, part, LANES - 1 :] == ag
        expo = ref[side, part, :]
        coef = (cot * (expo * per_total - jnp.where(match, per_count, 0.0))).astype(BF16)
        cosine = 1.0 + jnp.log(expo) * (1.0 / SCALE)
        return coef, jnp.sum(coef.astype(F32) * cosine, axis=1, keepdims=True)

    for k, part in enumerate(parts):
        for copy in ready[k]:
            copy.wait()
        coefs = []
        for side in range(2):
            mine, inner = coefficients(x_ref, side, part, factors[0])
            theirs, more = coefficients(y_ref, side, part, factors[1])
            coef_ref[side, part, :] = mine
            coefs.append((jnp.concatenate([mine, theirs], axis=1), inner + more))
        out.append(copies.start(coef_ref.at[:, part], coef_hbm.at[:, part]))
        if k == 0:
            extra_copy.wait()
            an_ref[n:, :n] = extra_ref[:n, :].astype(BF16)
            more_copy.wait()
            an_ref[n:, n:] = more_ref[...].astype(BF16)
            an_copy.wait()
        late[k].wait()
        grads = []
        for side, (coef, inner) in enumerate(coefs):
            dcn = jnp.dot(coef, an_ref[...], preferred_element_type=F32)
            inv = row_ref[side, part, :1]
            grads.append(inv * (dcn - cc_ref[side, part, :].astype(F32) * (inv * inner)))
        over, under = grads
        for b in range(own_ref.shape[0] // 2):
            top = over[:, b * LANES : (b + 1) * LANES]
            bottom = under[:, b * LANES : (b + 1) * LANES]
            own_ref[2 * b, part, :] = jnp.where(low, top, pltpu.roll(bottom, LANES // 2, 1))
            own_ref[2 * b + 1, part, :] = jnp.where(low, pltpu.roll(top, LANES // 2, 1), bottom)
        out.append(copies.start(own_ref.at[:, part], own_hbm.at[:, part]))
    for copy in out:
        copy.wait()


def candidate_stage(st, other, cot, ag, row, cc, an, x, y):
    n, cols = an.shape
    half = row.shape[0] // 2
    split = lambda v: v.reshape(2, half, -1)
    outs = [((2, half, n), BF16), ((2 * cols // LANES, half, LANES), F32)]
    scratch = [
        ((2, half, LANES), F32),
        ((2, half, cols), BF16),
        ((2, half, n), F32),
        ((2, half, n), F32),
        ((2 * n, cols), BF16),
        ((n + SPARE, n), F32),
        ((n, cols - n), F32),
    ]
    return pl.pallas_call(
        candidate_kernel,
        in_specs=[VMEM] * 4 + [HBM] * 5,
        out_specs=[VMEM, HBM, HBM],
        out_shape=[jax.ShapeDtypeStruct(*s) for s in [((1, n), F32)] + outs],
        scratch_shapes=[
            *(pltpu.VMEM(*s) for s in scratch + outs),
            pltpu.SemaphoreType.DMA((CANDIDATE_COPIES + 2 * CANDIDATE_STEPS,)),
        ],
        compiler_params=pltpu.CompilerParams(vmem_limit_bytes=60 * MIB),
        name="candidate_terms",
    )(st, other, cot, ag, split(row), split(cc), an, x, y)


def anchor_kernel(
    coef_hbm, row_hbm, c_hbm, xkeep, xsend, ykeep, ysend, coef_ref, row_ref, c_ref, scr, sems,
):
    copies = Copies(sems)
    share, cols = xkeep.shape[3:]
    row_copy = copies.start(row_hbm, row_ref)
    c_copies = [copies.start(c_hbm.at[:, pl.ds(h * cols, cols)], c_ref.at[h]) for h in range(2)]
    coef_copy = copies.start(coef_hbm, coef_ref)
    cand = lax.axis_index("cand")
    x0, y0 = cand % 2, (cand // NX) % 2

    out = []
    row_copy.wait()
    inv = row_ref[:, :1]
    for h, (keep, send) in enumerate(((xkeep, xsend), (ykeep, ysend))):
        c_copies[h].wait()
        cn = (c_ref[h].astype(F32) * inv).astype(BF16)
        if h == 0:
            coef_copy.wait()
        scr[h] = lax.dot_general(
            coef_ref[...], cn, (((0,), (0,)), ((), ())), preferred_element_type=F32
        ).reshape(scr.shape[1:])
        for other in range(2):
            if h == 0:
                y = y0 if other == 0 else 1 - y0
                mine, theirs = (y, x0), (y, 1 - x0)
            else:
                x = x0 if other == 0 else 1 - x0
                mine, theirs = (y0, x), (1 - y0, x)
            for (j, i), to in ((theirs, send), (mine, keep)):
                out.append(copies.start(scr.at[h, :, j, :, i], to.at[other]))
    for copy in out:
        copy.wait()


def anchor_stage(coef, row, candidates, share):
    m, width = candidates.shape
    n = coef.shape[1]
    cols = width // 2
    part = jax.ShapeDtypeStruct((2, NY // 2, NX // 2, share, cols), F32)
    return pl.pallas_call(
        anchor_kernel,
        in_specs=[HBM, HBM, HBM],
        out_specs=[HBM] * 4,
        out_shape=[part] * 4,
        scratch_shapes=[
            pltpu.VMEM((m, n), BF16),
            pltpu.VMEM((m, LANES), F32),
            pltpu.VMEM((2, m, cols), BF16),
            pltpu.VMEM((2, NY // 2, 2, NX // 2, 2, share, cols), F32),
            pltpu.SemaphoreType.DMA((12,)),
        ],
        compiler_params=pltpu.CompilerParams(vmem_limit_bytes=60 * MIB),
        cost_estimate=pl.CostEstimate(
            flops=2 * n * width * m, bytes_accessed=8 * MIB, transcendentals=0
        ),
        name="anchor_terms",
    )(coef, row, candidates)


def probe_kernel(t_ref, a_ref, o_ref):
    term = jnp.sum(t_ref[...], axis=0)
    values = a_ref[...].astype(F32)
    inv = inverse_radius(values)
    unit = values * inv
    o_ref[...] = (term - unit * jnp.sum(unit * term, axis=1, keepdims=True)) * inv


def probe_stage(terms, rows):
    return pl.pallas_call(
        probe_kernel,
        out_shape=jax.ShapeDtypeStruct(rows.shape, F32),
        compiler_params=pltpu.CompilerParams(vmem_limit_bytes=8 * MIB),
        name="probe_derivatives",
    )(terms, rows)


def unpack_kernel(p_ref, o_ref):
    half = p_ref.shape[0]
    t = p_ref[...].T
    o_ref[:, :half] = t[: LANES // 2]
    o_ref[:, half:] = t[LANES // 2 :]


def unpack_stage(packed):
    half = packed.shape[0]
    return pl.pallas_call(
        unpack_kernel,
        out_shape=jax.ShapeDtypeStruct((LANES // 2, 2 * half), F32),
        compiler_params=pltpu.CompilerParams(vmem_limit_bytes=62 * MIB),
        name="unpack",
    )(packed)


def per_device(n_anc, anchors, candidates, anchor_group, cand_group, cotangent):
    n, width = anchors.shape
    n_cand = NX * NY
    share = n // n_cand
    cand = lax.axis_index("cand")

    def swap(v, over_x):
        pairs = []
        for p in range(n_anc):
            for j in range(NY):
                for i in range(NX):
                    k = i if over_x else j
                    k += 1 if (k - p) % 2 == 0 else -1
                    to = j * NX + k % NX if over_x else (k % NY) * NX + i
                    pairs.append((p * n_cand + j * NX + i, p * n_cand + to))
        return lax.ppermute(v, ("anc", "cand"), pairs)

    def sibling(v):
        return lax.ppermute(v, "anc", [(p, p ^ 1) for p in range(n_anc)])

    ag, cg, cot = anchor_group.reshape(1, n), cand_group.reshape(1, -1), cotangent.reshape(1, n)
    an, mine, st, row, cc = score_stage(anchors, candidates, ag, cg, cot, n_cand)

    theirs = sibling(mine)
    st = jnp.sum(lax.all_to_all(st, "cand", 0, 0, tiled=True), axis=0)
    cost, coef, packed = candidate_stage(st, sibling(st), cot, ag, row, cc, an, mine, theirs)
    packed = lax.psum_scatter(
        packed, "anc", scatter_dimension=0,
        axis_index_groups=[list(range(c, n_anc, 2)) for c in range(2)], tiled=False,
    )
    grad_candidates = unpack_stage(packed).T

    xkeep, xsend, ykeep, ysend = anchor_stage(coef.reshape(-1, n), row, candidates, share)
    xgot, ygot = swap(xsend, True), swap(ysend, False)
    xagain, yagain = swap(xkeep[1] + xgot[1], False), swap(ykeep[1] + ygot[1], True)
    xpart, ypart = xkeep[0] + xgot[0] + xagain, ykeep[0] + ygot[0] + yagain
    groups = [
        [(2 * p + j) * NX + 2 * q + i for p in range(NY // 2) for q in range(NX // 2)]
        for j in range(2) for i in range(2)
    ]
    terms = jnp.concatenate([xpart, ypart], axis=-1).reshape(-1, share, width)
    terms = lax.all_to_all(terms, "cand", 0, 0, axis_index_groups=groups, tiled=True)
    rows = lax.dynamic_slice_in_dim(anchors, cand * share, share, 0)
    probe_derivatives = probe_stage(terms, rows)
    return cost.reshape(n), probe_derivatives, grad_candidates


def solution(mesh):
    in_specs = (P("anc", None), P("cand", None), P("anc"), P("cand"), P("anc"))
    out_specs = (P("anc"), P(("anc", "cand"), None), P("cand", "anc"))
    return jax.shard_map(
        functools.partial(per_device, mesh.shape["anc"]),
        mesh=mesh, in_specs=in_specs, out_specs=out_specs, check_vma=False,
    )
```

```python
import functools

import jax
import jax.numpy as jnp
from jax import lax
from jax.experimental import pallas as pl
from jax.experimental.pallas import tpu as pltpu
from jax.sharding import PartitionSpec as P

SCALE = 20.0
EPS = 1e-06
F32 = jnp.float32
BF16 = jnp.bfloat16
NX, NY = 4, 8
LANES = 128
SLOTS = 12
SPARE = 8
MIB = 2**20
VMEM = pl.BlockSpec(memory_space=pltpu.VMEM)
HBM = pl.BlockSpec(memory_space=pltpu.HBM)
SMEM = pl.BlockSpec(memory_space=pltpu.SMEM)


def inverse_radius(values):
    return 1.0 / jnp.sqrt(jnp.sum(values * values, axis=1, keepdims=True) + EPS)


class Copies:
    def __init__(self, sems):
        self.sems, self.all = sems, []

    def start(self, source, target):
        copy = pltpu.make_async_copy(source, target, self.sems.at[len(self.all)])
        copy.start()
        self.all.append(copy)
        return copy


def core_columns(values, core):
    side = (lax.broadcasted_iota(jnp.int32, (values.shape[0], LANES), 1) >= LANES // 2).astype(jnp.int32)
    stay = side == core
    blocks = []
    for k in range(0, values.shape[1], 2 * LANES):
        left, right = values[:, k : k + LANES], values[:, k + LANES : k + 2 * LANES]
        kept = jnp.where(core == 0, left, right)
        moved = jnp.where(core == 0, right, left)
        blocks.append(jnp.where(stay, kept, pltpu.roll(moved, LANES // 2, 1)))
    return blocks


SCORE_STEPS = 3
SCORE_COPIES = 3 + 4 * SCORE_STEPS


def score_kernel(
    a_hbm, c_hbm, ag_ref, cg_ref, cot_ref, an_hbm, x_hbm, st_hbm, row_hbm, cc_hbm,
    a_ref, c_ref, full_ref, an_ref, x_ref, st_ref, row_ref, cc_ref, acc_ref, sems,
):
    n, m = a_ref.shape[0], c_ref.shape[0]
    per = n // LANES
    core = lax.axis_index("anc") % 2
    rows = m // SCORE_STEPS
    parts = [pl.ds(k * rows, rows) for k in range(SCORE_STEPS)]
    copies = Copies(sems)
    a_parts = [pl.ds(r, LANES) for r in range(0, n, LANES)]
    a_copies = [copies.start(a_hbm.at[part], a_ref.at[part]) for part in a_parts]
    c_copies = [copies.start(c_hbm.at[part], c_ref.at[part]) for part in parts]
    out = []
    for k in range(0, m, LANES):
        size = min(LANES, m - k)
        row_ref[k : k + size, :] = jnp.broadcast_to(
            cg_ref[:, k : k + size].astype(F32), (LANES, size)
        ).T
    ag = ag_ref[...].astype(F32)
    x_ref[m + n : m + n + SPARE, :] = jnp.zeros((SPARE, n), F32)
    x_ref[m + n : m + n + 1, :] = ag
    x_ref[m + n + 1 : m + n + 2, :] = cot_ref[...]
    for r, a_copy in zip(range(0, n, LANES), a_copies):
        a_copy.wait()
        values = a_ref[r : r + LANES, :].astype(F32)
        unit = values * inverse_radius(values)
        full_ref[r : r + LANES, :] = unit.astype(BF16)
        for k, block in enumerate(core_columns(unit, core)):
            an_ref[r : r + LANES, k * LANES : (k + 1) * LANES] = block.astype(BF16)
        for k, block in enumerate(core_columns(unit, 1 - core)):
            first = m + r if k < per else m + n + SPARE + r
            k = k % per
            x_ref[first : first + LANES, k * LANES : (k + 1) * LANES] = block
    rest = pl.ds(m, x_ref.shape[0] - m)
    out.append(copies.start(x_ref.at[rest], x_hbm.at[rest]))
    out.append(copies.start(an_ref, an_hbm))
    left = lax.broadcasted_iota(jnp.int32, (rows, LANES), 1) < LANES // 2
    acc = None
    for part, c_copy in zip(parts, c_copies):
        c_copy.wait()
        values = c_ref[part, :].astype(F32)
        inv = inverse_radius(values)
        scores = SCALE * lax.dot_general(
            (values * inv).astype(BF16), full_ref[...], (((1,), (1,)), ((), ())),
            preferred_element_type=F32,
        )
        expo = jnp.exp(scores - SCALE)
        x_ref[part, :] = expo
        out.append(copies.start(x_ref.at[part], x_hbm.at[part]))
        group = row_ref[part, :]
        row_ref[part, :] = jnp.where(left, inv, group)
        out.append(copies.start(row_ref.at[part], row_hbm.at[part]))
        for k, block in enumerate(core_columns(values, core)):
            cc_ref[part, k * LANES : (k + 1) * LANES] = block.astype(BF16)
        out.append(copies.start(cc_ref.at[part], cc_hbm.at[part]))
        match = group[:, LANES - 1 :] == ag
        sums = (
            jnp.sum(expo, axis=0, keepdims=True),
            jnp.sum(jnp.where(match, 1.0, 0.0), axis=0, keepdims=True),
            jnp.sum(jnp.where(match, scores, 0.0), axis=0, keepdims=True),
        )
        acc = sums if acc is None else tuple(u + v for u, v in zip(acc, sums))
    for k, s in enumerate(acc):
        for j in range(per):
            acc_ref[k * per + j : k * per + j + 1, :] = s[:, j * LANES : (j + 1) * LANES]
    st_ref[...] = jnp.broadcast_to(acc_ref[...][None], st_ref.shape)
    out.append(copies.start(st_ref, st_hbm))
    for copy in out:
        copy.wait()


def score_stage(anchors, candidates, ag, cg, cot, copies):
    n, width = anchors.shape
    m = candidates.shape[0]
    shapes = [
        ((n, width // 2), BF16),
        ((m + 2 * n + SPARE, n), F32),
        ((copies, SLOTS, LANES), F32),
        ((m, LANES), F32),
        ((m, width // 2), BF16),
    ]
    return pl.pallas_call(
        score_kernel,
        in_specs=[HBM, HBM, VMEM, VMEM, VMEM],
        out_specs=[HBM] * 5,
        out_shape=[jax.ShapeDtypeStruct(*s) for s in shapes],
        scratch_shapes=[
            pltpu.VMEM((n, width), BF16),
            pltpu.VMEM((m, width), BF16),
            pltpu.VMEM((n, width), BF16),
            *(pltpu.VMEM(*s) for s in shapes),
            pltpu.VMEM((SLOTS, LANES), F32),
            pltpu.SemaphoreType.DMA((SCORE_COPIES + n // LANES,)),
        ],
        compiler_params=pltpu.CompilerParams(vmem_limit_bytes=62 * MIB),
        name="scores",
    )(anchors, candidates, ag, cg, cot)


CANDIDATE_STEPS = 3
CANDIDATE_COPIES = 4 + 6 * CANDIDATE_STEPS


def candidate_kernel(
    st_ref, other_ref, cot_ref, ag_ref, row_hbm, cc_hbm, an_hbm, x_hbm, y_hbm,
    cost_ref, coef_hbm, own_hbm,
    row_ref, cc_ref, x_ref, y_ref, an_ref, extra_ref, more_ref, coef_ref, own_ref, sems,
):
    n = ag_ref.shape[1]
    half = own_ref.shape[1]
    m = 2 * half
    rows = half // CANDIDATE_STEPS
    per = n // LANES
    wide = more_ref.shape[1]
    parts = [pl.ds(k * rows, rows) for k in range(CANDIDATE_STEPS)]
    copies = Copies(sems)
    spare_copy = copies.start(y_hbm.at[pl.ds(m + n, SPARE)], extra_ref.at[pl.ds(n, SPARE)])
    ready, late = [], []
    for k, part in enumerate(parts):
        ready.append([copies.start(row_hbm.at[:, part], row_ref.at[:, part])])
        for side in range(2):
            place = pl.ds(side * half + part.start, rows)
            ready[k].append(copies.start(x_hbm.at[place], x_ref.at[side, part]))
            ready[k].append(copies.start(y_hbm.at[place], y_ref.at[side, part]))
        if k == 0:
            an_copy = copies.start(an_hbm, an_ref.at[pl.ds(0, n)])
            extra_copy = copies.start(y_hbm.at[pl.ds(m, n)], extra_ref.at[pl.ds(0, n)])
            more_copy = copies.start(y_hbm.at[pl.ds(m + n + SPARE, n), pl.ds(0, wide)], more_ref)
        late.append(copies.start(cc_hbm.at[:, part], cc_ref.at[:, part]))
    out = []

    def sums(ref):
        st = ref[...]
        total, count, positive = (
            jnp.concatenate([st[k * per + j : k * per + j + 1, :] for j in range(per)], axis=1)
            for k in range(3)
        )
        return total, jnp.maximum(count, 1.0), positive

    total, count, positive = sums(st_ref)
    cost_ref[...] = SCALE + jnp.log(total) - positive / count
    spare_copy.wait()
    factors = [(SCALE * cot_ref[...], 1.0 / total, 1.0 / count, ag_ref[...].astype(F32))]
    total, count, _ = sums(other_ref)
    factors.append((SCALE * extra_ref[n + 1 : n + 2, :], 1.0 / total, 1.0 / count, extra_ref[n : n + 1, :]))
    low = lax.broadcasted_iota(jnp.int32, (rows, LANES), 1) < LANES // 2

    def coefficients(ref, side, part, factor):
        cot, per_total, per_count, ag = factor
        match = row_ref[side, part, LANES - 1 :] == ag
        expo = ref[side, part, :]
        coef = (cot * (expo * per_total - jnp.where(match, per_count, 0.0))).astype(BF16)
        cosine = 1.0 + jnp.log(expo) * (1.0 / SCALE)
        return coef, jnp.sum(coef.astype(F32) * cosine, axis=1, keepdims=True)

    for k, part in enumerate(parts):
        for copy in ready[k]:
            copy.wait()
        coefs = []
        for side in range(2):
            mine, inner = coefficients(x_ref, side, part, factors[0])
            theirs, more = coefficients(y_ref, side, part, factors[1])
            coef_ref[side, part, :] = mine
            coefs.append((jnp.concatenate([mine, theirs], axis=1), inner + more))
        out.append(copies.start(coef_ref.at[:, part], coef_hbm.at[:, part]))
        if k == 0:
            extra_copy.wait()
            an_ref[n:, :n] = extra_ref[:n, :].astype(BF16)
            more_copy.wait()
            an_ref[n:, n:] = more_ref[...].astype(BF16)
            an_copy.wait()
        late[k].wait()
        dcn = jnp.dot(
            jnp.concatenate([coef for coef, _ in coefs], axis=0), an_ref[...],
            preferred_element_type=F32,
        )
        grads = []
        for side, (_, inner) in enumerate(coefs):
            inv = row_ref[side, part, :1]
            term = dcn[side * rows : (side + 1) * rows]
            grads.append(inv * (term - cc_ref[side, part, :].astype(F32) * (inv * inner)))
        over, under = grads
        for b in range(own_ref.shape[0] // 2):
            top = over[:, b * LANES : (b + 1) * LANES]
            bottom = under[:, b * LANES : (b + 1) * LANES]
            own_ref[2 * b, part, :] = jnp.where(low, top, pltpu.roll(bottom, LANES // 2, 1))
            own_ref[2 * b + 1, part, :] = jnp.where(low, pltpu.roll(top, LANES // 2, 1), bottom)
        out.append(copies.start(own_ref.at[:, part], own_hbm.at[:, part]))
    for copy in out:
        copy.wait()


def candidate_stage(st, other, cot, ag, row, cc, an, x, y):
    n, cols = an.shape
    half = row.shape[0] // 2
    split = lambda v: v.reshape(2, half, -1)
    outs = [((2, half, n), BF16), ((2 * cols // LANES, half, LANES), F32)]
    scratch = [
        ((2, half, LANES), F32),
        ((2, half, cols), BF16),
        ((2, half, n), F32),
        ((2, half, n), F32),
        ((2 * n, cols), BF16),
        ((n + SPARE, n), F32),
        ((n, cols - n), F32),
    ]
    return pl.pallas_call(
        candidate_kernel,
        in_specs=[VMEM] * 4 + [HBM] * 5,
        out_specs=[VMEM, HBM, HBM],
        out_shape=[jax.ShapeDtypeStruct(*s) for s in [((1, n), F32)] + outs],
        scratch_shapes=[
            *(pltpu.VMEM(*s) for s in scratch + outs),
            pltpu.SemaphoreType.DMA((CANDIDATE_COPIES + 2 * CANDIDATE_STEPS,)),
        ],
        compiler_params=pltpu.CompilerParams(vmem_limit_bytes=60 * MIB),
        name="candidate_terms",
    )(st, other, cot, ag, split(row), split(cc), an, x, y)


def anchor_kernel(
    coef_hbm, row_hbm, c_hbm, xkeep, xsend, ykeep, ysend, coef_ref, row_ref, c_ref, scr, sems,
):
    copies = Copies(sems)
    share, cols = xkeep.shape[3:]
    row_copy = copies.start(row_hbm, row_ref)
    c_copies = [copies.start(c_hbm.at[:, pl.ds(h * cols, cols)], c_ref.at[h]) for h in range(2)]
    coef_copy = copies.start(coef_hbm, coef_ref)
    cand = lax.axis_index("cand")
    x0, y0 = cand % 2, (cand // NX) % 2

    out = []
    row_copy.wait()
    inv = row_ref[:, :1]
    for h, (keep, send) in enumerate(((xkeep, xsend), (ykeep, ysend))):
        c_copies[h].wait()
        cn = (c_ref[h].astype(F32) * inv).astype(BF16)
        if h == 0:
            coef_copy.wait()
        scr[h] = lax.dot_general(
            coef_ref[...], cn, (((0,), (0,)), ((), ())), preferred_element_type=F32
        ).reshape(scr.shape[1:])
        for other in range(2):
            if h == 0:
                y = y0 if other == 0 else 1 - y0
                mine, theirs = (y, x0), (y, 1 - x0)
            else:
                x = x0 if other == 0 else 1 - x0
                mine, theirs = (y0, x), (1 - y0, x)
            for (j, i), to in ((theirs, send), (mine, keep)):
                out.append(copies.start(scr.at[h, :, j, :, i], to.at[other]))
    for copy in out:
        copy.wait()


def anchor_stage(coef, row, candidates, share):
    m, width = candidates.shape
    n = coef.shape[1]
    cols = width // 2
    part = jax.ShapeDtypeStruct((2, NY // 2, NX // 2, share, cols), F32)
    return pl.pallas_call(
        anchor_kernel,
        in_specs=[HBM, HBM, HBM],
        out_specs=[HBM] * 4,
        out_shape=[part] * 4,
        scratch_shapes=[
            pltpu.VMEM((m, n), BF16),
            pltpu.VMEM((m, LANES), F32),
            pltpu.VMEM((2, m, cols), BF16),
            pltpu.VMEM((2, NY // 2, 2, NX // 2, 2, share, cols), F32),
            pltpu.SemaphoreType.DMA((12,)),
        ],
        compiler_params=pltpu.CompilerParams(vmem_limit_bytes=60 * MIB),
        cost_estimate=pl.CostEstimate(
            flops=2 * n * width * m, bytes_accessed=8 * MIB, transcendentals=0
        ),
        name="anchor_terms",
    )(coef, row, candidates)


def probe_kernel(t_ref, a_ref, o_ref):
    term = jnp.sum(t_ref[...], axis=0)
    values = a_ref[...].astype(F32)
    inv = inverse_radius(values)
    unit = values * inv
    o_ref[...] = (term - unit * jnp.sum(unit * term, axis=1, keepdims=True)) * inv


def probe_stage(terms, rows):
    return pl.pallas_call(
        probe_kernel,
        out_shape=jax.ShapeDtypeStruct(rows.shape, F32),
        compiler_params=pltpu.CompilerParams(vmem_limit_bytes=8 * MIB),
        name="probe_derivatives",
    )(terms, rows)


def unpack_kernel(p_ref, o_ref):
    half = p_ref.shape[0]
    t = p_ref[...].T
    o_ref[:, :half] = t[: LANES // 2]
    o_ref[:, half:] = t[LANES // 2 :]


def unpack_stage(packed):
    half = packed.shape[0]
    return pl.pallas_call(
        unpack_kernel,
        out_shape=jax.ShapeDtypeStruct((LANES // 2, 2 * half), F32),
        compiler_params=pltpu.CompilerParams(vmem_limit_bytes=62 * MIB),
        name="unpack",
    )(packed)


def per_device(n_anc, anchors, candidates, anchor_group, cand_group, cotangent):
    n, width = anchors.shape
    n_cand = NX * NY
    share = n // n_cand
    cand = lax.axis_index("cand")

    def swap(v, over_x):
        pairs = []
        for p in range(n_anc):
            for j in range(NY):
                for i in range(NX):
                    k = i if over_x else j
                    k += 1 if (k - p) % 2 == 0 else -1
                    to = j * NX + k % NX if over_x else (k % NY) * NX + i
                    pairs.append((p * n_cand + j * NX + i, p * n_cand + to))
        return lax.ppermute(v, ("anc", "cand"), pairs)

    def sibling(v):
        return lax.ppermute(v, "anc", [(p, p ^ 1) for p in range(n_anc)])

    ag, cg, cot = anchor_group.reshape(1, n), cand_group.reshape(1, -1), cotangent.reshape(1, n)
    an, mine, st, row, cc = score_stage(anchors, candidates, ag, cg, cot, n_cand)

    theirs = sibling(mine)
    st = jnp.sum(lax.all_to_all(st, "cand", 0, 0, tiled=True), axis=0)
    cost, coef, packed = candidate_stage(st, sibling(st), cot, ag, row, cc, an, mine, theirs)
    packed = lax.psum_scatter(
        packed, "anc", scatter_dimension=0,
        axis_index_groups=[list(range(c, n_anc, 2)) for c in range(2)], tiled=False,
    )
    grad_candidates = unpack_stage(packed).T

    xkeep, xsend, ykeep, ysend = anchor_stage(coef.reshape(-1, n), row, candidates, share)
    xgot, ygot = swap(xsend, True), swap(ysend, False)
    xagain, yagain = swap(xkeep[1] + xgot[1], False), swap(ykeep[1] + ygot[1], True)
    xpart, ypart = xkeep[0] + xgot[0] + xagain, ykeep[0] + ygot[0] + yagain
    groups = [
        [(2 * p + j) * NX + 2 * q + i for p in range(NY // 2) for q in range(NX // 2)]
        for j in range(2) for i in range(2)
    ]
    terms = jnp.concatenate([xpart, ypart], axis=-1).reshape(-1, share, width)
    terms = lax.all_to_all(terms, "cand", 0, 0, axis_index_groups=groups, tiled=True)
    rows = lax.dynamic_slice_in_dim(anchors, cand * share, share, 0)
    probe_derivatives = probe_stage(terms, rows)
    return cost.reshape(n), probe_derivatives, grad_candidates


def solution(mesh):
    in_specs = (P("anc", None), P("cand", None), P("anc"), P("cand"), P("anc"))
    out_specs = (P("anc"), P(("anc", "cand"), None), P("cand", "anc"))
    return jax.shard_map(
        functools.partial(per_device, mesh.shape["anc"]),
        mesh=mesh, in_specs=in_specs, out_specs=out_specs, check_vma=False,
    )
```

```python
import functools

import jax
import jax.numpy as jnp
from jax import lax
from jax.experimental import pallas as pl
from jax.experimental.pallas import tpu as pltpu
from jax.sharding import PartitionSpec as P

SCALE = 20.0
EPS = 1e-06
F32 = jnp.float32
BF16 = jnp.bfloat16
NX, NY = 4, 8
LANES = 128
SLOTS = 12
SPARE = 8
MIB = 2**20
VMEM = pl.BlockSpec(memory_space=pltpu.VMEM)
HBM = pl.BlockSpec(memory_space=pltpu.HBM)
SMEM = pl.BlockSpec(memory_space=pltpu.SMEM)


def inverse_radius(values):
    return 1.0 / jnp.sqrt(jnp.sum(values * values, axis=1, keepdims=True) + EPS)


class Copies:
    def __init__(self, sems):
        self.sems, self.all = sems, []

    def start(self, source, target):
        copy = pltpu.make_async_copy(source, target, self.sems.at[len(self.all)])
        copy.start()
        self.all.append(copy)
        return copy


def core_columns(values, core):
    side = (lax.broadcasted_iota(jnp.int32, (values.shape[0], LANES), 1) >= LANES // 2).astype(jnp.int32)
    stay = side == core
    blocks = []
    for k in range(0, values.shape[1], 2 * LANES):
        left, right = values[:, k : k + LANES], values[:, k + LANES : k + 2 * LANES]
        kept = jnp.where(core == 0, left, right)
        moved = jnp.where(core == 0, right, left)
        blocks.append(jnp.where(stay, kept, pltpu.roll(moved, LANES // 2, 1)))
    return blocks


SCORE_STEPS = 3
SCORE_COPIES = 4 + 4 * SCORE_STEPS


def score_kernel(
    a_hbm, c_hbm, ag_ref, cg_ref, cot_ref, an_hbm, x_hbm, st_hbm, row_hbm, cc_hbm,
    a_ref, c_ref, full_ref, an_ref, x_ref, st_ref, row_ref, cc_ref, acc_ref, sems,
):
    n, m = a_ref.shape[0], c_ref.shape[0]
    per = n // LANES
    core = lax.axis_index("anc") % 2
    rows = m // SCORE_STEPS
    parts = [pl.ds(k * rows, rows) for k in range(SCORE_STEPS)]
    copies = Copies(sems)
    a_parts = [pl.ds(r, LANES) for r in range(0, n, LANES)]
    a_copies = [copies.start(a_hbm.at[part], a_ref.at[part]) for part in a_parts]
    c_copies = [copies.start(c_hbm.at[part], c_ref.at[part]) for part in parts]
    out = []
    for k in range(0, m, LANES):
        size = min(LANES, m - k)
        row_ref[k : k + size, :] = jnp.broadcast_to(
            cg_ref[:, k : k + size].astype(F32), (LANES, size)
        ).T
    ag = ag_ref[...].astype(F32)
    x_ref[m + n : m + n + SPARE, :] = jnp.zeros((SPARE, n), F32)
    x_ref[m + n : m + n + 1, :] = ag
    x_ref[m + n + 1 : m + n + 2, :] = cot_ref[...]
    for r, a_copy in zip(range(0, n, LANES), a_copies):
        a_copy.wait()
        values = a_ref[r : r + LANES, :].astype(F32)
        unit = values * inverse_radius(values)
        full_ref[r : r + LANES, :] = unit.astype(BF16)
        for k, block in enumerate(core_columns(unit, core)):
            an_ref[r : r + LANES, k * LANES : (k + 1) * LANES] = block.astype(BF16)
        for k, block in enumerate(core_columns(unit, 1 - core)):
            first = m + r if k < per else m + n + SPARE + r
            k = k % per
            x_ref[first : first + LANES, k * LANES : (k + 1) * LANES] = block
    first = pl.ds(m, n + SPARE)
    out.append(copies.start(x_ref.at[first], x_hbm.at[first]))
    rest = (pl.ds(m + n + SPARE, n), pl.ds(0, an_ref.shape[1] - n))
    out.append(copies.start(x_ref.at[rest], x_hbm.at[rest]))
    out.append(copies.start(an_ref, an_hbm))
    left = lax.broadcasted_iota(jnp.int32, (rows, LANES), 1) < LANES // 2
    acc = None
    for part, c_copy in zip(parts, c_copies):
        c_copy.wait()
        values = c_ref[part, :].astype(F32)
        inv = inverse_radius(values)
        scores = SCALE * lax.dot_general(
            (values * inv).astype(BF16), full_ref[...], (((1,), (1,)), ((), ())),
            preferred_element_type=F32,
        )
        expo = jnp.exp(scores - SCALE)
        x_ref[part, :] = expo
        out.append(copies.start(x_ref.at[part], x_hbm.at[part]))
        group = row_ref[part, :]
        row_ref[part, :] = jnp.where(left, inv, group)
        out.append(copies.start(row_ref.at[part], row_hbm.at[part]))
        for k, block in enumerate(core_columns(values, core)):
            cc_ref[part, k * LANES : (k + 1) * LANES] = block.astype(BF16)
        out.append(copies.start(cc_ref.at[part], cc_hbm.at[part]))
        match = group[:, LANES - 1 :] == ag
        sums = (
            jnp.sum(expo, axis=0, keepdims=True),
            jnp.sum(jnp.where(match, 1.0, 0.0), axis=0, keepdims=True),
            jnp.sum(jnp.where(match, scores, 0.0), axis=0, keepdims=True),
        )
        acc = sums if acc is None else tuple(u + v for u, v in zip(acc, sums))
    for k, s in enumerate(acc):
        for j in range(per):
            acc_ref[k * per + j : k * per + j + 1, :] = s[:, j * LANES : (j + 1) * LANES]
    st_ref[...] = jnp.broadcast_to(acc_ref[...][None], st_ref.shape)
    out.append(copies.start(st_ref, st_hbm))
    for copy in out:
        copy.wait()


def score_stage(anchors, candidates, ag, cg, cot, copies):
    n, width = anchors.shape
    m = candidates.shape[0]
    shapes = [
        ((n, width // 2), BF16),
        ((m + 2 * n + SPARE, n), F32),
        ((copies, SLOTS, LANES), F32),
        ((m, LANES), F32),
        ((m, width // 2), BF16),
    ]
    return pl.pallas_call(
        score_kernel,
        in_specs=[HBM, HBM, VMEM, VMEM, VMEM],
        out_specs=[HBM] * 5,
        out_shape=[jax.ShapeDtypeStruct(*s) for s in shapes],
        scratch_shapes=[
            pltpu.VMEM((n, width), BF16),
            pltpu.VMEM((m, width), BF16),
            pltpu.VMEM((n, width), BF16),
            *(pltpu.VMEM(*s) for s in shapes),
            pltpu.VMEM((SLOTS, LANES), F32),
            pltpu.SemaphoreType.DMA((SCORE_COPIES + n // LANES,)),
        ],
        compiler_params=pltpu.CompilerParams(vmem_limit_bytes=62 * MIB),
        name="scores",
    )(anchors, candidates, ag, cg, cot)


CANDIDATE_STEPS = 3
CANDIDATE_COPIES = 4 + 6 * CANDIDATE_STEPS


def candidate_kernel(
    st_ref, other_ref, cot_ref, ag_ref, row_hbm, cc_hbm, an_hbm, x_hbm, y_hbm,
    cost_ref, coef_hbm, own_hbm,
    row_ref, cc_ref, x_ref, y_ref, an_ref, extra_ref, more_ref, coef_ref, own_ref, sems,
):
    n = ag_ref.shape[1]
    half = own_ref.shape[1]
    m = 2 * half
    rows = half // CANDIDATE_STEPS
    per = n // LANES
    wide = more_ref.shape[1]
    parts = [pl.ds(k * rows, rows) for k in range(CANDIDATE_STEPS)]
    copies = Copies(sems)
    spare_copy = copies.start(y_hbm.at[pl.ds(m + n, SPARE)], extra_ref.at[pl.ds(n, SPARE)])
    ready, late = [], []
    for k, part in enumerate(parts):
        ready.append([copies.start(row_hbm.at[:, part], row_ref.at[:, part])])
        for side in range(2):
            place = pl.ds(side * half + part.start, rows)
            ready[k].append(copies.start(x_hbm.at[place], x_ref.at[side, part]))
            ready[k].append(copies.start(y_hbm.at[place], y_ref.at[side, part]))
        if k == 0:
            an_copy = copies.start(an_hbm, an_ref.at[pl.ds(0, n)])
            extra_copy = copies.start(y_hbm.at[pl.ds(m, n)], extra_ref.at[pl.ds(0, n)])
            more_copy = copies.start(y_hbm.at[pl.ds(m + n + SPARE, n), pl.ds(0, wide)], more_ref)
        late.append(copies.start(cc_hbm.at[:, part], cc_ref.at[:, part]))
    out = []

    def sums(ref):
        st = ref[...]
        total, count, positive = (
            jnp.concatenate([st[k * per + j : k * per + j + 1, :] for j in range(per)], axis=1)
            for k in range(3)
        )
        return total, jnp.maximum(count, 1.0), positive

    total, count, positive = sums(st_ref)
    cost_ref[...] = SCALE + jnp.log(total) - positive / count
    spare_copy.wait()
    factors = [(SCALE * cot_ref[...], 1.0 / total, 1.0 / count, ag_ref[...].astype(F32))]
    total, count, _ = sums(other_ref)
    factors.append((SCALE * extra_ref[n + 1 : n + 2, :], 1.0 / total, 1.0 / count, extra_ref[n : n + 1, :]))
    low = lax.broadcasted_iota(jnp.int32, (rows, LANES), 1) < LANES // 2

    def coefficients(ref, side, part, factor):
        cot, per_total, per_count, ag = factor
        match = row_ref[side, part, LANES - 1 :] == ag
        expo = ref[side, part, :]
        coef = (cot * (expo * per_total - jnp.where(match, per_count, 0.0))).astype(BF16)
        cosine = 1.0 + jnp.log(expo) * (1.0 / SCALE)
        return coef, jnp.sum(coef.astype(F32) * cosine, axis=1, keepdims=True)

    for k, part in enumerate(parts):
        for copy in ready[k]:
            copy.wait()
        coefs = []
        for side in range(2):
            mine, inner = coefficients(x_ref, side, part, factors[0])
            theirs, more = coefficients(y_ref, side, part, factors[1])
            coef_ref[side, part, :] = mine
            coefs.append((jnp.concatenate([mine, theirs], axis=1), inner + more))
        out.append(copies.start(coef_ref.at[:, part], coef_hbm.at[:, part]))
        if k == 0:
            extra_copy.wait()
            an_ref[n:, :n] = extra_ref[:n, :].astype(BF16)
            more_copy.wait()
            an_ref[n:, n:] = more_ref[...].astype(BF16)
            an_copy.wait()
        late[k].wait()
        dcn = jnp.dot(
            jnp.concatenate([coef for coef, _ in coefs], axis=0), an_ref[...],
            preferred_element_type=F32,
        )
        grads = []
        for side, (_, inner) in enumerate(coefs):
            inv = row_ref[side, part, :1]
            term = dcn[side * rows : (side + 1) * rows]
            grads.append(inv * (term - cc_ref[side, part, :].astype(F32) * (inv * inner)))
        over, under = grads
        for b in range(own_ref.shape[0] // 2):
            top = over[:, b * LANES : (b + 1) * LANES]
            bottom = under[:, b * LANES : (b + 1) * LANES]
            own_ref[2 * b, part, :] = jnp.where(low, top, pltpu.roll(bottom, LANES // 2, 1))
            own_ref[2 * b + 1, part, :] = jnp.where(low, pltpu.roll(top, LANES // 2, 1), bottom)
        out.append(copies.start(own_ref.at[:, part], own_hbm.at[:, part]))
    for copy in out:
        copy.wait()


def candidate_stage(st, other, cot, ag, row, cc, an, x, y):
    n, cols = an.shape
    half = row.shape[0] // 2
    split = lambda v: v.reshape(2, half, -1)
    outs = [((2, half, n), BF16), ((2 * cols // LANES, half, LANES), F32)]
    scratch = [
        ((2, half, LANES), F32),
        ((2, half, cols), BF16),
        ((2, half, n), F32),
        ((2, half, n), F32),
        ((2 * n, cols), BF16),
        ((n + SPARE, n), F32),
        ((n, cols - n), F32),
    ]
    return pl.pallas_call(
        candidate_kernel,
        in_specs=[VMEM] * 4 + [HBM] * 5,
        out_specs=[VMEM, HBM, HBM],
        out_shape=[jax.ShapeDtypeStruct(*s) for s in [((1, n), F32)] + outs],
        scratch_shapes=[
            *(pltpu.VMEM(*s) for s in scratch + outs),
            pltpu.SemaphoreType.DMA((CANDIDATE_COPIES + 2 * CANDIDATE_STEPS,)),
        ],
        compiler_params=pltpu.CompilerParams(vmem_limit_bytes=32 * MIB),
        name="candidate_terms",
    )(st, other, cot, ag, split(row), split(cc), an, x, y)


def anchor_kernel(
    coef_hbm, row_hbm, c_hbm, xkeep, xsend, ykeep, ysend, coef_ref, row_ref, c_ref, scr, sems,
):
    copies = Copies(sems)
    share, cols = xkeep.shape[3:]
    row_copy = copies.start(row_hbm, row_ref)
    c_copies = [copies.start(c_hbm.at[:, pl.ds(h * cols, cols)], c_ref.at[h]) for h in range(2)]
    coef_copy = copies.start(coef_hbm, coef_ref)
    cand = lax.axis_index("cand")
    x0, y0 = cand % 2, (cand // NX) % 2

    out = []
    row_copy.wait()
    inv = row_ref[:, :1]
    for h, (keep, send) in enumerate(((xkeep, xsend), (ykeep, ysend))):
        c_copies[h].wait()
        cn = (c_ref[h].astype(F32) * inv).astype(BF16)
        if h == 0:
            coef_copy.wait()
        scr[h] = lax.dot_general(
            coef_ref[...], cn, (((0,), (0,)), ((), ())), preferred_element_type=F32
        ).reshape(scr.shape[1:])
        for other in range(2):
            if h == 0:
                y = y0 if other == 0 else 1 - y0
                mine, theirs = (y, x0), (y, 1 - x0)
            else:
                x = x0 if other == 0 else 1 - x0
                mine, theirs = (y0, x), (1 - y0, x)
            for (j, i), to in ((theirs, send), (mine, keep)):
                out.append(copies.start(scr.at[h, :, j, :, i], to.at[other]))
    for copy in out:
        copy.wait()


def anchor_stage(coef, row, candidates, share):
    m, width = candidates.shape
    n = coef.shape[1]
    cols = width // 2
    part = jax.ShapeDtypeStruct((2, NY // 2, NX // 2, share, cols), F32)
    return pl.pallas_call(
        anchor_kernel,
        in_specs=[HBM, HBM, HBM],
        out_specs=[HBM] * 4,
        out_shape=[part] * 4,
        scratch_shapes=[
            pltpu.VMEM((m, n), BF16),
            pltpu.VMEM((m, LANES), F32),
            pltpu.VMEM((2, m, cols), BF16),
            pltpu.VMEM((2, NY // 2, 2, NX // 2, 2, share, cols), F32),
            pltpu.SemaphoreType.DMA((12,)),
        ],
        compiler_params=pltpu.CompilerParams(vmem_limit_bytes=60 * MIB),
        cost_estimate=pl.CostEstimate(
            flops=2 * n * width * m, bytes_accessed=8 * MIB, transcendentals=0
        ),
        name="anchor_terms",
    )(coef, row, candidates)


def probe_kernel(t_ref, a_ref, o_ref):
    term = jnp.sum(t_ref[...], axis=0)
    values = a_ref[...].astype(F32)
    inv = inverse_radius(values)
    unit = values * inv
    o_ref[...] = (term - unit * jnp.sum(unit * term, axis=1, keepdims=True)) * inv


def probe_stage(terms, rows):
    return pl.pallas_call(
        probe_kernel,
        out_shape=jax.ShapeDtypeStruct(rows.shape, F32),
        compiler_params=pltpu.CompilerParams(vmem_limit_bytes=8 * MIB),
        name="probe_derivatives",
    )(terms, rows)


def unpack_kernel(p_ref, o_ref):
    half = p_ref.shape[0]
    t = p_ref[...].T
    o_ref[:, :half] = t[: LANES // 2]
    o_ref[:, half:] = t[LANES // 2 :]


def unpack_stage(packed):
    half = packed.shape[0]
    return pl.pallas_call(
        unpack_kernel,
        out_shape=jax.ShapeDtypeStruct((LANES // 2, 2 * half), F32),
        compiler_params=pltpu.CompilerParams(vmem_limit_bytes=62 * MIB),
        name="unpack",
    )(packed)


def per_device(n_anc, anchors, candidates, anchor_group, cand_group, cotangent):
    n, width = anchors.shape
    n_cand = NX * NY
    share = n // n_cand
    cand = lax.axis_index("cand")

    def swap(v, over_x):
        pairs = []
        for p in range(n_anc):
            for j in range(NY):
                for i in range(NX):
                    k = i if over_x else j
                    k += 1 if (k - p) % 2 == 0 else -1
                    to = j * NX + k % NX if over_x else (k % NY) * NX + i
                    pairs.append((p * n_cand + j * NX + i, p * n_cand + to))
        return lax.ppermute(v, ("anc", "cand"), pairs)

    def sibling(v):
        return lax.ppermute(v, "anc", [(p, p ^ 1) for p in range(n_anc)])

    ag, cg, cot = anchor_group.reshape(1, n), cand_group.reshape(1, -1), cotangent.reshape(1, n)
    an, mine, st, row, cc = score_stage(anchors, candidates, ag, cg, cot, n_cand)

    theirs = sibling(mine)
    st = jnp.sum(lax.all_to_all(st, "cand", 0, 0, tiled=True), axis=0)
    cost, coef, packed = candidate_stage(st, sibling(st), cot, ag, row, cc, an, mine, theirs)
    packed = lax.psum_scatter(
        packed, "anc", scatter_dimension=0,
        axis_index_groups=[list(range(c, n_anc, 2)) for c in range(2)], tiled=False,
    )
    grad_candidates = unpack_stage(packed).T

    xkeep, xsend, ykeep, ysend = anchor_stage(coef.reshape(-1, n), row, candidates, share)
    xgot, ygot = swap(xsend, True), swap(ysend, False)
    xagain, yagain = swap(xkeep[1] + xgot[1], False), swap(ykeep[1] + ygot[1], True)
    xpart, ypart = xkeep[0] + xgot[0] + xagain, ykeep[0] + ygot[0] + yagain
    groups = [
        [(2 * p + j) * NX + 2 * q + i for p in range(NY // 2) for q in range(NX // 2)]
        for j in range(2) for i in range(2)
    ]
    terms = jnp.concatenate([xpart, ypart], axis=-1).reshape(-1, share, width)
    terms = lax.all_to_all(terms, "cand", 0, 0, axis_index_groups=groups, tiled=True)
    rows = lax.dynamic_slice_in_dim(anchors, cand * share, share, 0)
    probe_derivatives = probe_stage(terms, rows)
    return cost.reshape(n), probe_derivatives, grad_candidates


def solution(mesh):
    in_specs = (P("anc", None), P("cand", None), P("anc"), P("cand"), P("anc"))
    out_specs = (P("anc"), P(("anc", "cand"), None), P("cand", "anc"))
    return jax.shard_map(
        functools.partial(per_device, mesh.shape["anc"]),
        mesh=mesh, in_specs=in_specs, out_specs=out_specs, check_vma=False,
    )
```

```python
import functools

import jax
import jax.numpy as jnp
from jax import lax
from jax.experimental import pallas as pl
from jax.experimental.pallas import tpu as pltpu
from jax.sharding import PartitionSpec as P

SCALE = 20.0
EPS = 1e-06
F32 = jnp.float32
BF16 = jnp.bfloat16
NX, NY = 4, 8
LANES = 128
SLOTS = 12
SPARE = 8
MIB = 2**20
VMEM = pl.BlockSpec(memory_space=pltpu.VMEM)
HBM = pl.BlockSpec(memory_space=pltpu.HBM)
SMEM = pl.BlockSpec(memory_space=pltpu.SMEM)


def inverse_radius(values):
    return 1.0 / jnp.sqrt(jnp.sum(values * values, axis=1, keepdims=True) + EPS)


class Copies:
    def __init__(self, sems):
        self.sems, self.all = sems, []

    def start(self, source, target):
        copy = pltpu.make_async_copy(source, target, self.sems.at[len(self.all)])
        copy.start()
        self.all.append(copy)
        return copy


def core_columns(values, core):
    side = (lax.broadcasted_iota(jnp.int32, (values.shape[0], LANES), 1) >= LANES // 2).astype(jnp.int32)
    stay = side == core
    blocks = []
    for k in range(0, values.shape[1], 2 * LANES):
        left, right = values[:, k : k + LANES], values[:, k + LANES : k + 2 * LANES]
        kept = jnp.where(core == 0, left, right)
        moved = jnp.where(core == 0, right, left)
        blocks.append(jnp.where(stay, kept, pltpu.roll(moved, LANES // 2, 1)))
    return blocks


SCORE_STEPS = 3
SCORE_COPIES = 4 + 4 * SCORE_STEPS


def score_kernel(
    a_hbm, c_hbm, ag_ref, cg_ref, cot_ref, an_hbm, x_hbm, st_hbm, row_hbm, cc_hbm,
    a_ref, c_ref, full_ref, an_ref, x_ref, st_ref, row_ref, cc_ref, acc_ref, sems,
):
    n, m = a_ref.shape[0], c_ref.shape[0]
    per = n // LANES
    core = lax.axis_index("anc") % 2
    rows = m // SCORE_STEPS
    parts = [pl.ds(k * rows, rows) for k in range(SCORE_STEPS)]
    copies = Copies(sems)
    a_parts = [pl.ds(r, LANES) for r in range(0, n, LANES)]
    a_copies = [copies.start(a_hbm.at[part], a_ref.at[part]) for part in a_parts]
    c_copies = [copies.start(c_hbm.at[part], c_ref.at[part]) for part in parts]
    out = []
    for k in range(0, m, LANES):
        size = min(LANES, m - k)
        row_ref[k : k + size, :] = jnp.broadcast_to(
            cg_ref[:, k : k + size].astype(F32), (LANES, size)
        ).T
    ag = ag_ref[...].astype(F32)
    x_ref[m + n : m + n + SPARE, :] = jnp.zeros((SPARE, n), F32)
    x_ref[m + n : m + n + 1, :] = ag
    x_ref[m + n + 1 : m + n + 2, :] = cot_ref[...]
    for r, a_copy in zip(range(0, n, LANES), a_copies):
        a_copy.wait()
        values = a_ref[r : r + LANES, :].astype(F32)
        unit = values * inverse_radius(values)
        full_ref[r : r + LANES, :] = unit.astype(BF16)
        for k, block in enumerate(core_columns(unit, core)):
            an_ref[r : r + LANES, k * LANES : (k + 1) * LANES] = block.astype(BF16)
        for k, block in enumerate(core_columns(unit, 1 - core)):
            first = m + r if k < per else m + n + SPARE + r
            k = k % per
            x_ref[first : first + LANES, k * LANES : (k + 1) * LANES] = block
    first = pl.ds(m, n + SPARE)
    out.append(copies.start(x_ref.at[first], x_hbm.at[first]))
    rest = (pl.ds(m + n + SPARE, n), pl.ds(0, an_ref.shape[1] - n))
    out.append(copies.start(x_ref.at[rest], x_hbm.at[rest]))
    out.append(copies.start(an_ref, an_hbm))
    left = lax.broadcasted_iota(jnp.int32, (rows, LANES), 1) < LANES // 2
    acc = None
    for part, c_copy in zip(parts, c_copies):
        c_copy.wait()
        values = c_ref[part, :].astype(F32)
        inv = inverse_radius(values)
        scores = SCALE * lax.dot_general(
            (values * inv).astype(BF16), full_ref[...], (((1,), (1,)), ((), ())),
            preferred_element_type=F32,
        )
        expo = jnp.exp(scores - SCALE)
        x_ref[part, :] = expo
        out.append(copies.start(x_ref.at[part], x_hbm.at[part]))
        group = row_ref[part, :]
        row_ref[part, :] = jnp.where(left, inv, group)
        out.append(copies.start(row_ref.at[part], row_hbm.at[part]))
        for k, block in enumerate(core_columns(values, core)):
            cc_ref[part, k * LANES : (k + 1) * LANES] = block.astype(BF16)
        out.append(copies.start(cc_ref.at[part], cc_hbm.at[part]))
        match = group[:, LANES - 1 :] == ag
        sums = (
            jnp.sum(expo, axis=0, keepdims=True),
            jnp.sum(jnp.where(match, 1.0, 0.0), axis=0, keepdims=True),
            jnp.sum(jnp.where(match, scores, 0.0), axis=0, keepdims=True),
        )
        acc = sums if acc is None else tuple(u + v for u, v in zip(acc, sums))
    for k, s in enumerate(acc):
        for j in range(per):
            acc_ref[k * per + j : k * per + j + 1, :] = s[:, j * LANES : (j + 1) * LANES]
    st_ref[...] = jnp.broadcast_to(acc_ref[...][None], st_ref.shape)
    out.append(copies.start(st_ref, st_hbm))
    for copy in out:
        copy.wait()


def score_stage(anchors, candidates, ag, cg, cot, copies):
    n, width = anchors.shape
    m = candidates.shape[0]
    shapes = [
        ((n, width // 2), BF16),
        ((m + 2 * n + SPARE, n), F32),
        ((copies, SLOTS, LANES), F32),
        ((m, LANES), F32),
        ((m, width // 2), BF16),
    ]
    return pl.pallas_call(
        score_kernel,
        in_specs=[HBM, HBM, VMEM, VMEM, VMEM],
        out_specs=[HBM] * 5,
        out_shape=[jax.ShapeDtypeStruct(*s) for s in shapes],
        scratch_shapes=[
            pltpu.VMEM((n, width), BF16),
            pltpu.VMEM((m, width), BF16),
            pltpu.VMEM((n, width), BF16),
            *(pltpu.VMEM(*s) for s in shapes),
            pltpu.VMEM((SLOTS, LANES), F32),
            pltpu.SemaphoreType.DMA((SCORE_COPIES + n // LANES,)),
        ],
        compiler_params=pltpu.CompilerParams(vmem_limit_bytes=62 * MIB),
        name="scores",
    )(anchors, candidates, ag, cg, cot)


CANDIDATE_STEPS = 3
CANDIDATE_COPIES = 4 + 6 * CANDIDATE_STEPS


def candidate_kernel(
    st_ref, other_ref, cot_ref, ag_ref, row_hbm, cc_hbm, an_hbm, x_hbm, y_hbm,
    cost_ref, coef_hbm, own_hbm,
    row_ref, cc_ref, x_ref, y_ref, an_ref, extra_ref, more_ref, coef_ref, own_ref, sems,
):
    n = ag_ref.shape[1]
    half = own_ref.shape[1]
    m = 2 * half
    rows = half // CANDIDATE_STEPS
    per = n // LANES
    wide = more_ref.shape[1]
    parts = [pl.ds(k * rows, rows) for k in range(CANDIDATE_STEPS)]
    copies = Copies(sems)
    spare_copy = copies.start(y_hbm.at[pl.ds(m + n, SPARE)], extra_ref.at[pl.ds(n, SPARE)])
    ready, late = [], []
    for k, part in enumerate(parts):
        ready.append([copies.start(row_hbm.at[:, part], row_ref.at[:, part])])
        for side in range(2):
            place = pl.ds(side * half + part.start, rows)
            ready[k].append(copies.start(x_hbm.at[place], x_ref.at[side, part]))
            ready[k].append(copies.start(y_hbm.at[place], y_ref.at[side, part]))
        if k == 0:
            an_copy = copies.start(an_hbm, an_ref.at[pl.ds(0, n)])
            extra_copy = copies.start(y_hbm.at[pl.ds(m, n)], extra_ref.at[pl.ds(0, n)])
            more_copy = copies.start(y_hbm.at[pl.ds(m + n + SPARE, n), pl.ds(0, wide)], more_ref)
        late.append(copies.start(cc_hbm.at[:, part], cc_ref.at[:, part]))
    out = []

    def sums(ref):
        st = ref[...]
        total, count, positive = (
            jnp.concatenate([st[k * per + j : k * per + j + 1, :] for j in range(per)], axis=1)
            for k in range(3)
        )
        return total, jnp.maximum(count, 1.0), positive

    total, count, positive = sums(st_ref)
    cost_ref[...] = SCALE + jnp.log(total) - positive / count
    spare_copy.wait()
    factors = [(SCALE * cot_ref[...], 1.0 / total, 1.0 / count, ag_ref[...].astype(F32))]
    total, count, _ = sums(other_ref)
    factors.append((SCALE * extra_ref[n + 1 : n + 2, :], 1.0 / total, 1.0 / count, extra_ref[n : n + 1, :]))
    low = lax.broadcasted_iota(jnp.int32, (rows, LANES), 1) < LANES // 2

    def coefficients(ref, side, part, factor):
        cot, per_total, per_count, ag = factor
        match = row_ref[side, part, LANES - 1 :] == ag
        expo = ref[side, part, :]
        coef = (cot * (expo * per_total - jnp.where(match, per_count, 0.0))).astype(BF16)
        cosine = 1.0 + jnp.log(expo) * (1.0 / SCALE)
        return coef, jnp.sum(coef.astype(F32) * cosine, axis=1, keepdims=True)

    for k, part in enumerate(parts):
        for copy in ready[k]:
            copy.wait()
        coefs = []
        for side in range(2):
            mine, inner = coefficients(x_ref, side, part, factors[0])
            theirs, more = coefficients(y_ref, side, part, factors[1])
            coef_ref[side, part, :] = mine
            coefs.append((jnp.concatenate([mine, theirs], axis=1), inner + more))
        out.append(copies.start(coef_ref.at[:, part], coef_hbm.at[:, part]))
        if k == 0:
            extra_copy.wait()
            an_ref[n:, :n] = extra_ref[:n, :].astype(BF16)
            more_copy.wait()
            an_ref[n:, n:] = more_ref[...].astype(BF16)
            an_copy.wait()
        late[k].wait()
        dcn = jnp.dot(
            jnp.concatenate([coef for coef, _ in coefs], axis=0), an_ref[...],
            preferred_element_type=F32,
        )
        grads = []
        for side, (_, inner) in enumerate(coefs):
            inv = row_ref[side, part, :1]
            term = dcn[side * rows : (side + 1) * rows]
            grads.append(inv * (term - cc_ref[side, part, :].astype(F32) * (inv * inner)))
        over, under = grads
        for b in range(own_ref.shape[0] // 2):
            top = over[:, b * LANES : (b + 1) * LANES]
            bottom = under[:, b * LANES : (b + 1) * LANES]
            own_ref[2 * b, part, :] = jnp.where(low, top, pltpu.roll(bottom, LANES // 2, 1))
            own_ref[2 * b + 1, part, :] = jnp.where(low, pltpu.roll(top, LANES // 2, 1), bottom)
        out.append(copies.start(own_ref.at[:, part], own_hbm.at[:, part]))
    for copy in out:
        copy.wait()


def candidate_stage(st, other, cot, ag, row, cc, an, x, y):
    n, cols = an.shape
    half = row.shape[0] // 2
    split = lambda v: v.reshape(2, half, -1)
    outs = [((2, half, n), BF16), ((2 * cols // LANES, half, LANES), F32)]
    scratch = [
        ((2, half, LANES), F32),
        ((2, half, cols), BF16),
        ((2, half, n), F32),
        ((2, half, n), F32),
        ((2 * n, cols), BF16),
        ((n + SPARE, n), F32),
        ((n, cols - n), F32),
    ]
    return pl.pallas_call(
        candidate_kernel,
        in_specs=[VMEM] * 4 + [HBM] * 5,
        out_specs=[VMEM, HBM, HBM],
        out_shape=[jax.ShapeDtypeStruct(*s) for s in [((1, n), F32)] + outs],
        scratch_shapes=[
            *(pltpu.VMEM(*s) for s in scratch + outs),
            pltpu.SemaphoreType.DMA((CANDIDATE_COPIES + 2 * CANDIDATE_STEPS,)),
        ],
        compiler_params=pltpu.CompilerParams(vmem_limit_bytes=62 * MIB),
        name="candidate_terms",
    )(st, other, cot, ag, split(row), split(cc), an, x, y)


def anchor_kernel(
    coef_hbm, row_hbm, c_hbm, xkeep, xsend, ykeep, ysend, coef_ref, row_ref, c_ref, scr, sems,
):
    copies = Copies(sems)
    share, cols = xkeep.shape[3:]
    row_copy = copies.start(row_hbm, row_ref)
    c_copies = [copies.start(c_hbm.at[:, pl.ds(h * cols, cols)], c_ref.at[h]) for h in range(2)]
    coef_copy = copies.start(coef_hbm, coef_ref)
    cand = lax.axis_index("cand")
    x0, y0 = cand % 2, (cand // NX) % 2

    out = []
    row_copy.wait()
    inv = row_ref[:, :1]
    for h, (keep, send) in enumerate(((xkeep, xsend), (ykeep, ysend))):
        c_copies[h].wait()
        cn = (c_ref[h].astype(F32) * inv).astype(BF16)
        if h == 0:
            coef_copy.wait()
        scr[h] = lax.dot_general(
            coef_ref[...], cn, (((0,), (0,)), ((), ())), preferred_element_type=F32
        ).reshape(scr.shape[1:])
        for other in range(2):
            if h == 0:
                y = y0 if other == 0 else 1 - y0
                mine, theirs = (y, x0), (y, 1 - x0)
            else:
                x = x0 if other == 0 else 1 - x0
                mine, theirs = (y0, x), (1 - y0, x)
            for (j, i), to in ((theirs, send), (mine, keep)):
                out.append(copies.start(scr.at[h, :, j, :, i], to.at[other]))
    for copy in out:
        copy.wait()


def anchor_stage(coef, row, candidates, share):
    m, width = candidates.shape
    n = coef.shape[1]
    cols = width // 2
    part = jax.ShapeDtypeStruct((2, NY // 2, NX // 2, share, cols), F32)
    return pl.pallas_call(
        anchor_kernel,
        in_specs=[HBM, HBM, HBM],
        out_specs=[HBM] * 4,
        out_shape=[part] * 4,
        scratch_shapes=[
            pltpu.VMEM((m, n), BF16),
            pltpu.VMEM((m, LANES), F32),
            pltpu.VMEM((2, m, cols), BF16),
            pltpu.VMEM((2, NY // 2, 2, NX // 2, 2, share, cols), F32),
            pltpu.SemaphoreType.DMA((12,)),
        ],
        compiler_params=pltpu.CompilerParams(vmem_limit_bytes=60 * MIB),
        cost_estimate=pl.CostEstimate(
            flops=2 * n * width * m, bytes_accessed=8 * MIB, transcendentals=0
        ),
        name="anchor_terms",
    )(coef, row, candidates)


def probe_kernel(t_ref, a_ref, o_ref):
    term = jnp.sum(t_ref[...], axis=0)
    values = a_ref[...].astype(F32)
    inv = inverse_radius(values)
    unit = values * inv
    o_ref[...] = (term - unit * jnp.sum(unit * term, axis=1, keepdims=True)) * inv


def probe_stage(terms, rows):
    return pl.pallas_call(
        probe_kernel,
        out_shape=jax.ShapeDtypeStruct(rows.shape, F32),
        compiler_params=pltpu.CompilerParams(vmem_limit_bytes=8 * MIB),
        name="probe_derivatives",
    )(terms, rows)


def unpack_kernel(p_ref, o_ref):
    half = p_ref.shape[0]
    t = p_ref[...].T
    o_ref[:, :half] = t[: LANES // 2]
    o_ref[:, half:] = t[LANES // 2 :]


def unpack_stage(packed):
    half = packed.shape[0]
    return pl.pallas_call(
        unpack_kernel,
        out_shape=jax.ShapeDtypeStruct((LANES // 2, 2 * half), F32),
        compiler_params=pltpu.CompilerParams(vmem_limit_bytes=62 * MIB),
        name="unpack",
    )(packed)


def per_device(n_anc, anchors, candidates, anchor_group, cand_group, cotangent):
    n, width = anchors.shape
    n_cand = NX * NY
    share = n // n_cand
    cand = lax.axis_index("cand")

    def swap(v, over_x):
        pairs = []
        for p in range(n_anc):
            for j in range(NY):
                for i in range(NX):
                    k = i if over_x else j
                    k += 1 if (k - p) % 2 == 0 else -1
                    to = j * NX + k % NX if over_x else (k % NY) * NX + i
                    pairs.append((p * n_cand + j * NX + i, p * n_cand + to))
        return lax.ppermute(v, ("anc", "cand"), pairs)

    def sibling(v):
        return lax.ppermute(v, "anc", [(p, p ^ 1) for p in range(n_anc)])

    ag, cg, cot = anchor_group.reshape(1, n), cand_group.reshape(1, -1), cotangent.reshape(1, n)
    an, mine, st, row, cc = score_stage(anchors, candidates, ag, cg, cot, n_cand)

    theirs = sibling(mine)
    st = jnp.sum(lax.all_to_all(st, "cand", 0, 0, tiled=True), axis=0)
    cost, coef, packed = candidate_stage(st, sibling(st), cot, ag, row, cc, an, mine, theirs)
    packed = lax.psum_scatter(
        packed, "anc", scatter_dimension=0,
        axis_index_groups=[list(range(c, n_anc, 2)) for c in range(2)], tiled=False,
    )
    grad_candidates = unpack_stage(packed).T

    xkeep, xsend, ykeep, ysend = anchor_stage(coef.reshape(-1, n), row, candidates, share)
    xgot, ygot = swap(xsend, True), swap(ysend, False)
    xagain, yagain = swap(xkeep[1] + xgot[1], False), swap(ykeep[1] + ygot[1], True)
    xpart, ypart = xkeep[0] + xgot[0] + xagain, ykeep[0] + ygot[0] + yagain
    groups = [
        [(2 * p + j) * NX + 2 * q + i for p in range(NY // 2) for q in range(NX // 2)]
        for j in range(2) for i in range(2)
    ]
    terms = jnp.concatenate([xpart, ypart], axis=-1).reshape(-1, share, width)
    terms = lax.all_to_all(terms, "cand", 0, 0, axis_index_groups=groups, tiled=True)
    rows = lax.dynamic_slice_in_dim(anchors, cand * share, share, 0)
    probe_derivatives = probe_stage(terms, rows)
    return cost.reshape(n), probe_derivatives, grad_candidates


def solution(mesh):
    in_specs = (P("anc", None), P("cand", None), P("anc"), P("cand"), P("anc"))
    out_specs = (P("anc"), P(("anc", "cand"), None), P("cand", "anc"))
    return jax.shard_map(
        functools.partial(per_device, mesh.shape["anc"]),
        mesh=mesh, in_specs=in_specs, out_specs=out_specs, check_vma=False,
    )
```
